512 devices in a mesh: fsdp: 8 (over y_hi, x), shard: 64 (over y_lo, z, core).
Axes of the slice: x: 4, y: 4 (y_hi: 2, y_lo: 2; y = y_hi * 2 + y_lo), z: 16, core: 2. Of those that a mesh axis runs over, the one named last changes fastest.
Arguments:
- query_momentum: float32 [256, 294912], P('fsdp', 'shard')
- key_value_momentum: float32 [256, 131072], P('fsdp', 'shard')
- query_blocks: bfloat16 [256, 294912], P('fsdp', 'shard'), may hold values from -6 to 6
- key_value_blocks: bfloat16 [256, 131072], P('fsdp', 'shard'), may hold values from -6 to 6
- clip_flags: int32 [256], P('fsdp'), may hold values 0 or 1
- logit_max: float32 [256], P('fsdp'), may hold values from 25 to 400
Outputs:
- q_updated: bfloat16 [256, 294912], P(None, 'shard')
- kv_updated: bfloat16 [256, 131072], P(None, 'shard')
The draws below stay inside these ranges and needn't reach their ends.
All inputs are finite; a program needn't handle non-finite values. No bound on the sum of `clip_flags` on one device may be relied on, other than what follows from the above.
Results may differ from the reference program's by a relative error of at most 0.004.
Values may be sent and summed in bfloat16 or wider, within the bound.
A program may use at most 64 MiB of HBM per device.

```python
import math
import jax
import jax.numpy as jnp
from jax import lax

PLAIN_FEATURES = 128
ROTARY_FEATURES = 64
VALUE_FEATURES = 128
QUERY_RANK = 1536
KEY_VALUE_RANK = 512
NS_ITERS = 5
HEAD_BLOCK_TOTAL = 256
QF = 294912
KF = 131072


def rescaled_blocks(key, count, rows, cols, spread):
    keys = jax.random.split(key, 4)
    normal_part = jax.random.normal(keys[0], (count, rows, cols), jnp.float32)
    base = normal_part
    row_scale = jnp.exp(jax.random.uniform(keys[2], (count, rows, 1), jnp.float32) * jnp.log(spread))
    col_scale = jnp.exp(jax.random.uniform(keys[3], (count, 1, cols), jnp.float32) * jnp.log(spread))
    return (base * row_scale * col_scale).reshape(count, rows * cols)


def draw_query_momentum(key, part):
    key = jax.random.fold_in(key, 11)
    return rescaled_blocks(key, HEAD_BLOCK_TOTAL, PLAIN_FEATURES + ROTARY_FEATURES, QUERY_RANK, 10.0)


def draw_key_value_momentum(key, part):
    key = jax.random.fold_in(key, 23)
    return rescaled_blocks(key, HEAD_BLOCK_TOTAL, PLAIN_FEATURES + VALUE_FEATURES, KEY_VALUE_RANK, 10.0)


def plant(entries, rng, least, largest):
    extent = entries.shape
    place = [jax.random.randint(jax.random.fold_in(rng, axis), (), 0, extent[axis]) for axis in range(len(extent))]
    entries = entries.at[tuple(place)].set(least)
    longest = extent.index(max(extent))
    place[longest] = (place[longest] + 1) % extent[longest]
    return entries.at[tuple(place)].set(largest)


def steps_of(key, shape, shards, least, high):
    factor_of = 1.0
    for dim, parts in shards:
        draws = jax.random.uniform(jax.random.fold_in(jax.random.fold_in(key, 6), dim), (parts,), jnp.float32, least / len(shards), high / len(shards))
        factor_of = factor_of * jnp.repeat(jnp.exp(draws), shape[dim] // parts).reshape((-1,) + (1,) * (len(shape) - 1 - dim))
    return factor_of


def noise(stream_key, shape, scale, reach, pieces=(), kind=jnp.bfloat16):
    drawn = jax.random.normal(stream_key, shape, jnp.float32) * scale
    if len(pieces) > 0:
        drawn = steps_of(stream_key, shape, pieces, -0.22, 0.18) * drawn
    return jnp.clip(drawn, min=-reach, max=reach).astype(kind)


def setup_inputs(seed: int = 0) -> dict:
    seeds = jax.random.split(jax.random.key(seed), 7)
    return {
        "query_momentum": draw_query_momentum(jax.random.fold_in(seeds[6], 71), 0),
        "key_value_momentum": draw_key_value_momentum(jax.random.fold_in(seeds[6], 71), 0),
        "query_blocks": noise(seeds[2], (HEAD_BLOCK_TOTAL, QF), 1.0, 6.0, ((0, 8), (1, 64))),
        "key_value_blocks": noise(seeds[3], (HEAD_BLOCK_TOTAL, KF), 1.0, 6.0, ((0, 8), (1, 64))),
        "clip_flags": plant((jax.random.randint(seeds[4], (HEAD_BLOCK_TOTAL,), 0, 4) < 3).astype(jnp.int32), jax.random.fold_in(seeds[4], 1), 0, 1),
        "logit_max": jnp.clip(jnp.exp(math.log(400.0) - 2.7725887 * jax.random.uniform(seeds[5], (HEAD_BLOCK_TOTAL,), jnp.float32) ** steps_of(seeds[5], (HEAD_BLOCK_TOTAL,), ((0, 8),), -0.2, 0.2)), 25.0, 400.0),
    }


COEF_A = 3.4445
COEF_B = -4.775
COEF_C = 2.0315
CLIP_TAU = 100.0
LEARNING_RATE = 0.5
DECAY_WEIGHT = 0.1

def make_orthogonal(matrix):
    frobenius = jnp.sqrt(jnp.sum(matrix * matrix))
    iterate = matrix / (frobenius + 1e-07)
    for sweep in range(NS_ITERS):
        gram_matrix = jnp.dot(iterate, iterate.T, precision=lax.Precision.HIGHEST)
        polynomial = COEF_B * gram_matrix + COEF_C * jnp.dot(gram_matrix, gram_matrix, precision=lax.Precision.HIGHEST)
        iterate = COEF_A * iterate + jnp.dot(polynomial, iterate, precision=lax.Precision.HIGHEST)
    return iterate.astype(jnp.bfloat16)

def reference(query_momentum, key_value_momentum, query_blocks, key_value_blocks, clip_flags, logit_max):
    eta = jnp.where(clip_flags > 0, jnp.minimum(jnp.float32(1.0), CLIP_TAU / logit_max), jnp.float32(1.0))
    root = jnp.sqrt(eta)
    query_row_list = PLAIN_FEATURES + ROTARY_FEATURES
    key_value_row_list = PLAIN_FEATURES + VALUE_FEATURES
    query_update_step = lax.map(lambda flattened: make_orthogonal(flattened.reshape(query_row_list, QUERY_RANK)), query_momentum)
    key_value_update = lax.map(lambda flattened: make_orthogonal(flattened.reshape(key_value_row_list, KEY_VALUE_RANK)), key_value_momentum)
    query_index = jnp.arange(query_row_list, dtype=jnp.int32)
    keyval_index = jnp.arange(key_value_row_list, dtype=jnp.int32)
    query_scale_factor = jnp.where(query_index[None, :] < PLAIN_FEATURES, root[:, None], eta[:, None])[:, :, None]
    key_value_scale = jnp.where(keyval_index[None, :] < PLAIN_FEATURES, root[:, None], jnp.float32(1.0))[:, :, None]
    query_weight_matrix = query_blocks.reshape(query_blocks.shape[0], query_row_list, QUERY_RANK).astype(jnp.float32)
    key_value_weight = key_value_blocks.reshape(key_value_blocks.shape[0], key_value_row_list, KEY_VALUE_RANK).astype(jnp.float32)
    query_fresh = query_scale_factor * (query_weight_matrix * (1.0 - LEARNING_RATE * DECAY_WEIGHT) - LEARNING_RATE * 0.2 * math.sqrt(QUERY_RANK) * query_update_step.astype(jnp.float32))
    key_value_fresh = key_value_scale * (key_value_weight * (1.0 - LEARNING_RATE * DECAY_WEIGHT) - LEARNING_RATE * 0.2 * math.sqrt(KEY_VALUE_RANK) * key_value_update.astype(jnp.float32))
    return (query_fresh.astype(jnp.bfloat16).reshape(query_blocks.shape), key_value_fresh.astype(jnp.bfloat16).reshape(key_value_blocks.shape))
```

```python
import functools
import math
from types import SimpleNamespace

import jax
import jax.numpy as jnp
from jax import lax
from jax.experimental import pallas as pl
from jax.experimental.pallas import tpu as pltpu
from jax.sharding import PartitionSpec as P

COEF_A = 3.4445
COEF_B = -4.775
COEF_C = 2.0315
CLIP_TAU = 100.0
LEARNING_RATE = 0.5
DECAY_WEIGHT = 0.1
NS_ITERS = 5
PLAIN = 128

F32 = jnp.float32
BF16 = jnp.bfloat16
Z = 16
LANE = 128
X_RING = 4
MESH = pl.DeviceIdType.MESH


def make_kind(name, rows, rank, chunks):
    slabs = rank // LANE
    per_chunk = slabs // chunks
    sources = 4 * rows
    return SimpleNamespace(
        name=name,
        rows=rows,
        rank=rank,
        chunks=chunks,
        slabs=slabs,
        per_chunk=per_chunk,
        sources=sources,
        message=sources * per_chunk,
        size=Z * sources,
        piece=rows * rank,
        strip=rows * per_chunk * LANE,
        span=per_chunk * LANE,
        back_rows=rows // chunks,
    )


QUERY = make_kind("q", 3, 1536, 3)
KEYVAL = make_kind("kv", 4, 512, 2)
KINDS = (QUERY, KEYVAL)


def scratch_of(kind):
    g = kind.chunks
    dma = pltpu.SemaphoreType.DMA
    return dict(
        raw=pltpu.VMEM((32, kind.piece), F32),
        mom=pltpu.VMEM((g, 32, kind.strip), BF16),
        gather=pltpu.VMEM((g, 4, 16, kind.strip), BF16),
        weights=pltpu.VMEM((4, 16, kind.piece), BF16),
        turn=pltpu.VMEM((Z * kind.message, LANE), F32),
        out_z=pltpu.VMEM((g, Z * kind.message, LANE), BF16),
        in_z=pltpu.VMEM((g, Z * kind.message, LANE), BF16),
        back_out=pltpu.VMEM((g, Z * kind.message, LANE), BF16),
        back_in=pltpu.VMEM((g, Z * kind.message, LANE), BF16),
        matrix=pltpu.VMEM((kind.size, kind.rank), BF16),
        strips=pltpu.VMEM((g, 4, 16, kind.strip), BF16),
        r_raw=dma((1,)),
        s_gather=dma((g,)),
        r_gather=dma((g,)),
        s_weights=dma((1,)),
        r_weights=dma((1,)),
        s_z=dma((g,)),
        r_z=dma((g,)),
        s_back=dma((g,)),
        r_back=dma((g,)),
        s_y=dma((g,)),
        r_y=dma((g,)),
        s_x=dma((g,)),
        r_x=dma((g, 2)),
        r_relay=dma((g, 2)),
    )


NAMES = tuple(scratch_of(QUERY))


def split(value):
    high = value.astype(BF16)
    return high, (value - high.astype(F32)).astype(BF16)


def dot(left, right):
    return jnp.dot(left, right, preferred_element_type=F32)


def product(left, right):
    return dot(left[0], right[0]) + (dot(left[0], right[1]) + dot(left[1], right[0]))


def identity(size):
    first = lax.broadcasted_iota(jnp.int32, (size, size), 0)
    second = lax.broadcasted_iota(jnp.int32, (size, size), 1)
    return first == second


def newton_schulz(gram, size):
    diagonal = identity(size)
    square = jnp.sum(jnp.where(diagonal, gram, 0.0), axis=(0, 1), keepdims=True)
    inverse = 1.0 / (jnp.sqrt(square) + 1e-07)
    a = (gram * inverse) * inverse
    total = None
    for step in range(NS_ITERS):
        a_parts = split(a)
        poly = COEF_B * a + COEF_C * product(a_parts, a_parts)
        poly = jnp.where(diagonal, poly + COEF_A, poly)
        parts = split(poly)
        total = poly if total is None else product(parts, split(total))
        if step < NS_ITERS - 1:
            a = product(parts, split(product(parts, a_parts)))
    return total * inverse


def kernel(q_mom, kv_mom, q_weights, kv_weights, flags_in, logit_in, q_out, kv_out, *scratch):
    flags, logit, small_sems, *scratch = scratch
    fsdp = lax.axis_index("fsdp")
    shard = lax.axis_index("shard")
    y_hi, x = fsdp // X_RING, fsdp % X_RING
    y, z, core = shard // 32, (shard // 2) % Z, shard % 2
    me = y * 2 + core
    half = len(NAMES)
    q = SimpleNamespace(
        k=QUERY, m=q_mom, w=q_weights, out=q_out, **dict(zip(NAMES, scratch[:half]))
    )
    kv = SimpleNamespace(
        k=KEYVAL, m=kv_mom, w=kv_weights, out=kv_out, **dict(zip(NAMES, scratch[half:]))
    )
    both = (q, kv)

    def place(to_y, to_z, to_core):
        return to_y * 32 + to_z * 2 + to_core

    def send(source, target, s_sem, r_sem, device):
        pltpu.make_async_remote_copy(
            src_ref=source,
            dst_ref=target,
            send_sem=s_sem,
            recv_sem=r_sem,
            device_id=device,
            device_id_type=MESH,
        ).start()

    def keep(source, target, sem):
        pltpu.make_async_copy(source, target, sem).start()

    def wait(ref, sem):
        pltpu.make_async_copy(ref, ref, sem).wait()

    x_right = y_hi * X_RING + (x + 1) % X_RING
    x_left = y_hi * X_RING + (x + X_RING - 1) % X_RING
    other = (1 - y_hi) * X_RING + x

    for ref in both:
        pltpu.make_async_copy(ref.m, ref.raw, ref.r_raw.at[0]).start()
    small = ((flags_in, flags, small_sems.at[0]), (logit_in, logit, small_sems.at[1]))
    for source, target, sem in small:
        pltpu.make_async_copy(source, target, sem).start()
    barrier = pltpu.get_barrier_semaphore()

    def greet(to_fsdp, to_shard):
        pl.semaphore_signal(barrier, inc=1, device_id=(to_fsdp, to_shard), device_id_type=MESH)

    greet(fsdp, place(y, z, 1 - core))
    greet(fsdp, place(1 - y, z, core))
    greet(fsdp, place(1 - y, z, 1 - core))
    for to_y in (y, 1 - y):
        for to_core in (core, 1 - core):
            greet(other, place(to_y, z, to_core))
    greet(x_right, shard)
    greet(x_left, shard)

    def greet_z(step, carry):
        greet(fsdp, place(y, (z + step) % Z, core))
        return carry

    lax.fori_loop(1, Z, greet_z, 0)

    for ref in both:
        k = ref.k
        pltpu.make_async_copy(ref.m, ref.raw, ref.r_raw.at[0]).wait()
        for g in range(k.chunks):
            for r in range(k.rows):
                start = (r * k.slabs + g * k.per_chunk) * LANE
                ref.mom[g, :, r * k.span : (r + 1) * k.span] = ref.raw[
                    :, start : start + k.span
                ].astype(BF16)

    pl.semaphore_wait(barrier, 24)

    def to_group(ref, to_core, source, target, s_sem, r_sem):
        @pl.when(core == to_core)
        def _():
            keep(source(y), target, r_sem)

        @pl.when(core != to_core)
        def _():
            send(source(y), target, s_sem, r_sem, (fsdp, place(y, z, to_core)))

        send(source(1 - y), target, s_sem, r_sem, (fsdp, place(1 - y, z, to_core)))

    def rows16(to_y):
        return pl.ds(pl.multiple_of(to_y * 16, 16), 16)

    for g in range(max(k.chunks for k in KINDS)):
        for to_core, ref in enumerate(both):
            if g < ref.k.chunks:
                to_group(
                    ref,
                    to_core,
                    lambda to_y, ref=ref, g=g: ref.mom.at[g, rows16(to_y), :],
                    ref.gather.at[g, me],
                    ref.s_gather.at[g],
                    ref.r_gather.at[g],
                )
    for to_core, ref in enumerate(both):
        to_group(
            ref,
            to_core,
            lambda to_y, ref=ref: ref.w.at[rows16(to_y), :],
            ref.weights.at[me],
            ref.s_weights.at[0],
            ref.r_weights.at[0],
        )

    def z_send(k, source, target, s_sem, r_sem):
        def one(i, carry):
            far = jnp.where(i % 2 == 1, 8 - (i + 1) // 2, 8 + i // 2)
            to_z = (z + far) % Z
            start = pl.multiple_of(to_z * k.message, 16)
            send(
                source.at[pl.ds(start, k.message), :],
                target.at[pl.ds(pl.multiple_of(z * k.message, 16), k.message), :],
                s_sem,
                r_sem,
                (fsdp, place(y, to_z, core)),
            )
            return carry

        lax.fori_loop(0, Z - 1, one, 0)
        here = pl.ds(pl.multiple_of(z * k.message, 16), k.message)
        keep(source.at[here, :], target.at[here, :], r_sem)

    def every(k, offset):
        return pl.ds(offset, 16, stride=k.message)

    def exchange(ref):
        k = ref.k
        for g in range(k.chunks):
            wait(ref.gather.at[g], ref.r_gather.at[g])
            for s in range(4):
                for r in range(k.rows):
                    for c in range(k.per_chunk):
                        start = (r * k.per_chunk + c) * LANE
                        tile = ref.gather[g, s, :, start : start + LANE]
                        ref.turn[every(k, c * k.sources + r * 4 + s), :] = tile.astype(F32)
            ref.out_z[g] = ref.turn[...].astype(BF16)
            z_send(k, ref.out_z.at[g], ref.in_z.at[g], ref.s_z.at[g], ref.r_z.at[g])

    def orthogonalize(ref):
        k = ref.k
        gram = None
        for g in range(k.chunks):
            wait(ref.in_z.at[g], ref.r_z.at[g])
            ref.turn[...] = ref.in_z[g].astype(F32)
            for c in range(k.per_chunk):
                column = (g * k.per_chunk + c) * LANE
                for n in range(k.sources):
                    tile = ref.turn[every(k, c * k.sources + n), :]
                    ref.matrix[n * 16 : n * 16 + 16, column : column + LANE] = tile.astype(BF16)
            part = ref.matrix[:, g * k.span : (g + 1) * k.span]
            term = lax.dot_general(
                part, part, (((1,), (1,)), ((), ())), preferred_element_type=F32
            )
            gram = term if gram is None else gram + term
        high, low = split(newton_schulz(gram, k.size))
        for g in range(k.chunks):
            rows = k.back_rows * 4
            own = slice(g * rows * 16, (g + 1) * rows * 16)
            whole = ref.matrix[...]
            update = dot(high[own], whole) + dot(low[own], whole)
            for n in range(rows):
                for c in range(k.slabs):
                    ref.turn[every(k, n * k.slabs + c), :] = update[
                        n * 16 : n * 16 + 16, c * LANE : (c + 1) * LANE
                    ]
            ref.back_out[g] = ref.turn[...].astype(BF16)
            z_send(k, ref.back_out.at[g], ref.back_in.at[g], ref.s_back.at[g], ref.r_back.at[g])

    def scales():
        ratio = jnp.minimum(1.0, CLIP_TAU / logit[...])
        eta_row = jnp.where(flags[...] > 0, ratio, 1.0)
        spread = jnp.where(identity(32), jnp.broadcast_to(eta_row, (32, 32)), 0.0)
        column = jnp.sum(spread, axis=1, keepdims=True)
        eta = jnp.where(y == 0, column[:16], column[16:])
        return jnp.broadcast_to(eta, (16, LANE)), jnp.broadcast_to(jnp.sqrt(eta), (16, LANE))

    def part(ref, g, start, count):
        rows = pl.ds(pl.multiple_of(start, 16), count)
        return ref.out.at[rows, g * ref.k.strip : (g + 1) * ref.k.strip]

    def renew(ref, g, eta, root):
        k = ref.k
        wait(ref.back_in.at[g], ref.r_back.at[g])
        ref.turn[...] = ref.back_in[g].astype(F32)
        tail = eta if k is QUERY else jnp.ones_like(eta)
        for r in range(k.back_rows):
            for s in range(4):
                row = ((s // 2) * 32 + z * 2 + s % 2) * k.rows + g * k.back_rows + r
                scale = jnp.where(row < PLAIN, root, tail)
                for c in range(k.slabs):
                    update = ref.turn[every(k, (r * 4 + s) * k.slabs + c), :]
                    start = (r * k.slabs + c) * LANE
                    column = g * k.strip + start
                    old = ref.weights[s, :, column : column + LANE].astype(F32)
                    fresh = scale * (
                        old * (1.0 - LEARNING_RATE * DECAY_WEIGHT)
                        - LEARNING_RATE * 0.2 * math.sqrt(k.rank) * update
                    )
                    ref.strips[g, s, :, start : start + LANE] = fresh.astype(BF16)
        mine = part(ref, g, fsdp * 32 + y * 16, 16)
        sems = ref.s_y.at[g], ref.r_y.at[g]
        for to_core in (core, 1 - core):
            strip = ref.strips.at[g, y * 2 + to_core]
            send(strip, mine, *sems, (other, place(y, z, to_core)))
            strip = ref.strips.at[g, (1 - y) * 2 + to_core]
            send(strip, mine, *sems, (fsdp, place(1 - y, z, to_core)))
            send(strip, mine, *sems, (other, place(1 - y, z, to_core)))
        send(ref.strips.at[g, y * 2 + 1 - core], mine, *sems, (fsdp, place(y, z, 1 - core)))
        keep(ref.strips.at[g, me], mine, ref.r_y.at[g])

    def block(ref, g, from_y_hi, from_x):
        start = (from_y_hi * X_RING + from_x) * 32
        return part(ref, g, start, 32)

    def along_x(ref, g):
        wait(part(ref, g, 0, 64), ref.r_y.at[g])
        for h in range(2):
            rows = block(ref, g, h, x)
            send(rows, rows, ref.s_x.at[g], ref.r_x.at[g, 0], (x_right, shard))
            send(rows, rows, ref.s_x.at[g], ref.r_x.at[g, 1], (x_left, shard))

    def relay(ref, g):
        wait(part(ref, g, 0, 64), ref.r_x.at[g, 0])
        rows = block(ref, g, 0, (x + X_RING - 1) % X_RING)
        send(rows, rows, ref.s_x.at[g], ref.r_relay.at[g, 0], (x_right, shard))
        wait(part(ref, g, 0, 64), ref.r_x.at[g, 1])
        rows = block(ref, g, 1, (x + 1) % X_RING)
        send(rows, rows, ref.s_x.at[g], ref.r_relay.at[g, 1], (x_left, shard))

    def run(ref):
        k = ref.k
        exchange(ref)
        orthogonalize(ref)
        for source, target, sem in small:
            pltpu.make_async_copy(source, target, sem).wait()
        eta, root = scales()
        wait(ref.weights, ref.r_weights.at[0])
        if k is KEYVAL:
            renew(kv, 0, eta, root)
            renew(kv, 1, eta, root)
        along_x(kv, 0)
        along_x(kv, 1)
        for g in range(3):
            if k is QUERY:
                renew(q, g, eta, root)
            if g == 0:
                relay(kv, 0)
                relay(kv, 1)
            along_x(q, g)
            if g > 0:
                relay(q, g - 1)
        relay(q, 2)
        for g in range(k.chunks):
            wait(part(ref, g, 0, 112), ref.s_y.at[g])
            most = pl.ds(0, (Z - 1) * k.message)
            wait(ref.out_z.at[g, most, :], ref.s_z.at[g])
            wait(ref.back_out.at[g, most, :], ref.s_back.at[g])
            wait(ref.mom.at[g, pl.ds(0, 16), :], ref.s_gather.at[g])
        wait(ref.weights.at[0], ref.s_weights.at[0])
        away = kv if ref is q else q
        for g in range(away.k.chunks):
            wait(away.mom.at[g], away.s_gather.at[g])
        wait(away.weights.at[pl.ds(0, 2)], away.s_weights.at[0])

    pl.when(core == 0)(lambda: run(q))
    pl.when(core == 1)(lambda: run(kv))

    for ref in both:
        for g in range(ref.k.chunks):
            wait(part(ref, g, 0, 32), ref.r_relay.at[g, 0])
            wait(part(ref, g, 0, 32), ref.r_relay.at[g, 1])
            wait(part(ref, g, 0, 192), ref.s_x.at[g])


def per_device(
    query_momentum, key_value_momentum, query_blocks, key_value_blocks, clip_flags, logit_max
):
    hbm = pl.BlockSpec(memory_space=pltpu.HBM)
    anywhere = pl.BlockSpec(memory_space=pl.ANY)
    scratch = [
        pltpu.VMEM((1, 32), jnp.int32),
        pltpu.VMEM((1, 32), F32),
        pltpu.SemaphoreType.DMA((2,)),
    ]
    for k in KINDS:
        scratch += list(scratch_of(k).values())
    return pl.pallas_call(
        kernel,
        name="muon",
        out_shape=tuple(pltpu.VMEM((256, k.piece), BF16) for k in KINDS),
        in_specs=[hbm] * 6,
        out_specs=(anywhere, anywhere),
        scratch_shapes=scratch,
        compiler_params=pltpu.CompilerParams(
            collective_id=0, has_side_effects=True, vmem_limit_bytes=60 * 1024 * 1024
        ),
    )(
        query_momentum,
        key_value_momentum,
        query_blocks,
        key_value_blocks,
        clip_flags.reshape(1, 32),
        logit_max.reshape(1, 32),
    )


def solution(mesh):
    placed = (
        P("fsdp", "shard"),
        P("fsdp", "shard"),
        P("fsdp", "shard"),
        P("fsdp", "shard"),
        P("fsdp"),
        P("fsdp"),
    )
    return jax.shard_map(
        per_device,
        mesh=mesh,
        in_specs=placed,
        out_specs=(P(None, "shard"), P(None, "shard")),
        check_vma=False,
    )
```

```python
import functools
import math
from types import SimpleNamespace

import jax
import jax.numpy as jnp
from jax import lax
from jax.experimental import pallas as pl
from jax.experimental.pallas import tpu as pltpu
from jax.sharding import PartitionSpec as P

COEF_A = 3.4445
COEF_B = -4.775
COEF_C = 2.0315
CLIP_TAU = 100.0
LEARNING_RATE = 0.5
DECAY_WEIGHT = 0.1
NS_ITERS = 5
PLAIN = 128

F32 = jnp.float32
BF16 = jnp.bfloat16
Z = 16
LANE = 128
X_RING = 4
MESH = pl.DeviceIdType.MESH


def make_kind(name, rows, rank, chunks, back):
    slabs = rank // LANE
    per_chunk = slabs // chunks
    sources = 4 * rows
    return SimpleNamespace(
        name=name,
        rows=rows,
        rank=rank,
        chunks=chunks,
        slabs=slabs,
        per_chunk=per_chunk,
        sources=sources,
        message=sources * per_chunk,
        size=Z * sources,
        piece=rows * rank,
        strip=rows * per_chunk * LANE,
        span=per_chunk * LANE,
        back=tuple((sum(back[:i]), n) for i, n in enumerate(back)),
    )


UNIT = 512
QUERY = make_kind("q", 3, 1536, 3, (3, 3, 2, 1))
KEYVAL = make_kind("kv", 4, 512, 2, (2, 2))
KINDS = (QUERY, KEYVAL)


def scratch_of(kind):
    g, b = kind.chunks, len(kind.back)
    back_size = Z * 4 * kind.piece // LANE
    dma = pltpu.SemaphoreType.DMA
    return dict(
        raw=pltpu.VMEM((32, kind.piece), F32),
        mom=pltpu.VMEM((g, 32, kind.strip), BF16),
        gather=pltpu.VMEM((g, 4, 16, kind.strip), BF16),
        weights=pltpu.VMEM((4, 16, kind.piece), BF16),
        turn=pltpu.VMEM((Z * kind.message, LANE), F32),
        out_z=pltpu.VMEM((g, Z * kind.message, LANE), BF16),
        in_z=pltpu.VMEM((g, Z * kind.message, LANE), BF16),
        back_out=pltpu.VMEM((back_size, LANE), BF16),
        back_in=pltpu.VMEM((back_size, LANE), BF16),
        matrix=pltpu.VMEM((kind.size, kind.rank), BF16),
        strips=pltpu.VMEM((4, 16, kind.piece), BF16),
        r_raw=dma((1,)),
        cross=pltpu.VMEM((2, 2, 16, kind.piece), BF16),
        s_cross=dma((b,)),
        r_cross=dma((b, 2)),
        s_pass=dma((b,)),
        r_pass=dma((b, 2)),
        s_gather=dma((g,)),
        r_gather=dma((g,)),
        s_weights=dma((1,)),
        r_weights=dma((1,)),
        s_z=dma((g,)),
        r_z=dma((g,)),
        s_back=dma((b,)),
        r_back=dma((b,)),
        s_y=dma((b,)),
        r_y=dma((b,)),
        s_x=dma((b,)),
        r_x=dma((b, 2)),
        r_relay=dma((b, 2)),
    )


NAMES = tuple(scratch_of(QUERY))


def split(value):
    high = value.astype(BF16)
    return high, (value - high.astype(F32)).astype(BF16)


def dot(left, right):
    return jnp.dot(left, right, preferred_element_type=F32)


def products(lefts, right):
    high, low = right
    size = high.shape[0]
    by_high = dot(jnp.concatenate([term for left in lefts for term in left], axis=0), high)
    by_low = dot(jnp.concatenate([left[0] for left in lefts], axis=0), low)
    results = []
    for i in range(len(lefts)):
        first, second = 2 * i * size, (2 * i + 1) * size
        small = by_high[second : second + size] + by_low[i * size : (i + 1) * size]
        results.append(by_high[first : first + size] + small)
    return results


def identity(size):
    first = lax.broadcasted_iota(jnp.int32, (size, size), 0)
    second = lax.broadcasted_iota(jnp.int32, (size, size), 1)
    return first == second


def newton_schulz(gram, size):
    diagonal = identity(size)
    square = jnp.sum(jnp.where(diagonal, gram, 0.0), axis=(0, 1), keepdims=True)
    inverse = 1.0 / (jnp.sqrt(square) + 1e-07)
    a = (gram * inverse) * inverse
    total = None
    for step in range(NS_ITERS):
        a_parts = split(a)
        poly = COEF_B * a + COEF_C * products([a_parts], a_parts)[0]
        poly = jnp.where(diagonal, poly + COEF_A, poly)
        parts = split(poly)
        lefts = [a_parts] if step < NS_ITERS - 1 else []
        if total is not None:
            lefts.append(split(total))
        results = products(lefts, parts)
        total = poly if total is None else results.pop()
        if results:
            a = products([split(results[0])], parts)[0]
    return total * inverse


def kernel(q_mom, kv_mom, q_weights, kv_weights, flags_in, logit_in, q_out, kv_out, *scratch):
    flags, logit, small_sems, *scratch = scratch
    fsdp = lax.axis_index("fsdp")
    shard = lax.axis_index("shard")
    y_hi, x = fsdp // X_RING, fsdp % X_RING
    y, z, core = shard // 32, (shard // 2) % Z, shard % 2
    me = y * 2 + core
    half = len(NAMES)
    q = SimpleNamespace(
        k=QUERY, m=q_mom, w=q_weights, out=q_out, **dict(zip(NAMES, scratch[:half]))
    )
    kv = SimpleNamespace(
        k=KEYVAL, m=kv_mom, w=kv_weights, out=kv_out, **dict(zip(NAMES, scratch[half:]))
    )
    both = (q, kv)

    def place(to_y, to_z, to_core):
        return to_y * 32 + to_z * 2 + to_core

    def send(source, target, s_sem, r_sem, device):
        pltpu.make_async_remote_copy(
            src_ref=source,
            dst_ref=target,
            send_sem=s_sem,
            recv_sem=r_sem,
            device_id=device,
            device_id_type=MESH,
        ).start()

    def keep(source, target, sem):
        pltpu.make_async_copy(source, target, sem).start()

    def wait(ref, sem):
        pltpu.make_async_copy(ref, ref, sem).wait()

    x_right = y_hi * X_RING + (x + 1) % X_RING
    x_left = y_hi * X_RING + (x + X_RING - 1) % X_RING
    other = (1 - y_hi) * X_RING + x

    for ref in both:
        pltpu.make_async_copy(ref.m, ref.raw, ref.r_raw.at[0]).start()
    small = ((flags_in, flags, small_sems.at[0]), (logit_in, logit, small_sems.at[1]))
    for source, target, sem in small:
        pltpu.make_async_copy(source, target, sem).start()
    barrier = pltpu.get_barrier_semaphore()

    def greet(to_fsdp, to_shard):
        pl.semaphore_signal(barrier, inc=1, device_id=(to_fsdp, to_shard), device_id_type=MESH)

    greet(fsdp, place(y, z, 1 - core))
    greet(fsdp, place(1 - y, z, core))
    greet(fsdp, place(1 - y, z, 1 - core))
    for to_y in (y, 1 - y):
        for to_core in (core, 1 - core):
            greet(other, place(to_y, z, to_core))
    greet(x_right, shard)
    greet(x_left, shard)

    def greet_z(step, carry):
        greet(fsdp, place(y, (z + step) % Z, core))
        return carry

    lax.fori_loop(1, Z, greet_z, 0)

    for ref in both:
        k = ref.k
        pltpu.make_async_copy(ref.m, ref.raw, ref.r_raw.at[0]).wait()
        for g in range(k.chunks):
            for r in range(k.rows):
                start = (r * k.slabs + g * k.per_chunk) * LANE
                ref.mom[g, :, r * k.span : (r + 1) * k.span] = ref.raw[
                    :, start : start + k.span
                ].astype(BF16)

    pl.semaphore_wait(barrier, 24)

    def to_group(ref, to_core, source, target, s_sem, r_sem):
        @pl.when(core == to_core)
        def _():
            keep(source(y), target, r_sem)

        @pl.when(core != to_core)
        def _():
            send(source(y), target, s_sem, r_sem, (fsdp, place(y, z, to_core)))

        send(source(1 - y), target, s_sem, r_sem, (fsdp, place(1 - y, z, to_core)))

    def rows16(to_y):
        return pl.ds(pl.multiple_of(to_y * 16, 16), 16)

    def gather(g):
        for to_core, ref in enumerate(both):
            if g < ref.k.chunks:
                to_group(
                    ref,
                    to_core,
                    lambda to_y, ref=ref: ref.mom.at[g, rows16(to_y), :],
                    ref.gather.at[g, me],
                    ref.s_gather.at[g],
                    ref.r_gather.at[g],
                )

    def gathered(own, g):
        for ref in both:
            if g < ref.k.chunks:
                strips = ref.mom.at[g, pl.ds(0, 16), :] if ref is own else ref.mom.at[g]
                wait(strips, ref.s_gather.at[g])

    def send_weights():
        for to_core, ref in enumerate(both):
            to_group(
                ref,
                to_core,
                lambda to_y, ref=ref: ref.w.at[rows16(to_y), :],
                ref.weights.at[me],
                ref.s_weights.at[0],
                ref.r_weights.at[0],
            )

    def z_send(rows, source, target, s_sem, r_sem):
        def one(i, carry):
            far = jnp.where(i % 2 == 1, 8 - (i + 1) // 2, 8 + i // 2)
            to_z = (z + far) % Z
            start = pl.multiple_of(to_z * rows, 16)
            send(
                source.at[pl.ds(start, rows), :],
                target.at[pl.ds(pl.multiple_of(z * rows, 16), rows), :],
                s_sem,
                r_sem,
                (fsdp, place(y, to_z, core)),
            )
            return carry

        lax.fori_loop(0, Z - 1, one, 0)
        here = pl.ds(pl.multiple_of(z * rows, 16), rows)
        keep(source.at[here, :], target.at[here, :], r_sem)

    def every(rows, offset):
        return pl.ds(offset, 16, stride=rows)

    def exchange(ref):
        k = ref.k
        rounds = max(kind.chunks for kind in KINDS)
        gather(0)
        for g in range(rounds):
            gathered(ref, g)
            if g + 1 < rounds:
                gather(g + 1)
            if g >= k.chunks:
                continue
            wait(ref.gather.at[g], ref.r_gather.at[g])
            for s in range(4):
                for r in range(k.rows):
                    for c in range(k.per_chunk):
                        start = (r * k.per_chunk + c) * LANE
                        tile = ref.gather[g, s, :, start : start + LANE]
                        ref.turn[every(k.message, c * k.sources + r * 4 + s), :] = tile.astype(F32)
            ref.out_z[g] = ref.turn[...].astype(BF16)
            z_send(k.message, ref.out_z.at[g], ref.in_z.at[g], ref.s_z.at[g], ref.r_z.at[g])

    def orthogonalize(ref):
        k = ref.k
        gram = None
        for g in range(k.chunks):
            wait(ref.in_z.at[g], ref.r_z.at[g])
            ref.turn[...] = ref.in_z[g].astype(F32)
            for c in range(k.per_chunk):
                column = (g * k.per_chunk + c) * LANE
                for n in range(k.sources):
                    tile = ref.turn[every(k.message, c * k.sources + n), :]
                    ref.matrix[n * 16 : n * 16 + 16, column : column + LANE] = tile.astype(BF16)
            part = ref.matrix[:, g * k.span : (g + 1) * k.span]
            term = lax.dot_general(
                part, part, (((1,), (1,)), ((), ())), preferred_element_type=F32
            )
            gram = term if gram is None else gram + term
        return split(newton_schulz(gram, k.size))

    def prepare(ref, terms, g):
        k = ref.k
        high, low = terms
        first, units = k.back[g]
        for i in range(units):
            row, column = divmod((first + i) * UNIT, k.rank)
            own = slice(row * 64, row * 64 + 64)
            both_terms = jnp.concatenate([high[own], low[own]], axis=0)
            both_terms = dot(both_terms, ref.matrix[:, column : column + UNIT])
            update = both_terms[:64] + both_terms[64:]
            for n in range(4):
                for c in range(4):
                    ref.turn[every(units * 16, i * 16 + n * 4 + c), :] = update[
                        n * 16 : n * 16 + 16, c * LANE : (c + 1) * LANE
                    ]
        ref.back_out[back_span(first, units), :] = ref.turn[: Z * units * 16].astype(BF16)

    def start_back(ref, g):
        first, units = ref.k.back[g]
        span = back_span(first, units)
        sems = ref.s_back.at[g], ref.r_back.at[g]
        z_send(units * 16, ref.back_out.at[span, :], ref.back_in.at[span, :], *sems)

    def left_back(ref, g):
        units = ref.k.back[g][1]
        wait(ref.back_out.at[pl.ds(0, (Z - 1) * 16 * units), :], ref.s_back.at[g])

    def back_span(first, units):
        return pl.ds(Z * 16 * first, Z * 16 * units)

    sides = (
        (x_right, lax.rem(x + X_RING - 1, X_RING)),
        (x_left, lax.rem(x + 1, X_RING)),
    )

    def scales():
        ratio = jnp.minimum(1.0, CLIP_TAU / logit[...])
        eta_row = jnp.where(flags[...] > 0, ratio, 1.0)
        spread = jnp.where(identity(32), jnp.broadcast_to(eta_row, (32, 32)), 0.0)
        column = jnp.sum(spread, axis=1, keepdims=True)
        eta = jnp.where(y == 0, column[:16], column[16:])
        return jnp.broadcast_to(eta, (16, LANE)), jnp.broadcast_to(jnp.sqrt(eta), (16, LANE))

    def part(ref, g, start, count):
        rows = pl.ds(pl.multiple_of(start, 16), count)
        return ref.out.at[rows, chunk_columns(ref, g)]

    def chunk_columns(ref, g):
        first, units = ref.k.back[g]
        return slice(first * UNIT, (first + units) * UNIT)

    def renew(ref, g, eta, root):
        k = ref.k
        first, units = k.back[g]
        span = back_span(first, units)
        wait(ref.back_in.at[span, :], ref.r_back.at[g])
        ref.turn[: Z * units * 16] = ref.back_in[span, :].astype(F32)
        tail = eta if k is QUERY else jnp.ones_like(eta)
        for i in range(units):
            for s in range(4):
                row = (first + i) * UNIT // k.rank
                row = ((s // 2) * 32 + z * 2 + s % 2) * k.rows + row
                scale = jnp.where(row < PLAIN, root, tail)
                for c in range(4):
                    update = ref.turn[every(units * 16, i * 16 + s * 4 + c), :]
                    column = (first + i) * UNIT + c * LANE
                    old = ref.weights[s, :, column : column + LANE].astype(F32)
                    fresh = scale * (
                        old * (1.0 - LEARNING_RATE * DECAY_WEIGHT)
                        - LEARNING_RATE * 0.2 * math.sqrt(k.rank) * update
                    )
                    ref.strips[s, :, column : column + LANE] = fresh.astype(BF16)
        columns = chunk_columns(ref, g)
        mine = part(ref, g, fsdp * 32 + y * 16, 16)
        pair = ref.strips.at[pl.ds(pl.multiple_of((1 - y) * 2, 2), 2), :, columns]
        for side, (to_fsdp, _) in enumerate(sides):
            target = ref.cross.at[side, :, :, columns]
            send(pair, target, ref.s_cross.at[g], ref.r_cross.at[g, side], (to_fsdp, shard))
        sems = ref.s_y.at[g], ref.r_y.at[g]
        for to_core in (core, 1 - core):
            strip = ref.strips.at[y * 2 + to_core, :, columns]
            send(strip, mine, *sems, (other, place(y, z, to_core)))
            strip = ref.strips.at[(1 - y) * 2 + to_core, :, columns]
            send(strip, mine, *sems, (fsdp, place(1 - y, z, to_core)))
            send(strip, mine, *sems, (other, place(1 - y, z, to_core)))
        strip = ref.strips.at[y * 2 + 1 - core, :, columns]
        send(strip, mine, *sems, (fsdp, place(y, z, 1 - core)))
        keep(ref.strips.at[me, :, columns], mine, ref.r_y.at[g])

    def pass_on(ref, g):
        columns = chunk_columns(ref, g)
        for side, (_, from_x) in enumerate(sides):
            landed = ref.cross.at[side, :, :, columns]
            wait(landed, ref.r_cross.at[g, side])
            target = part(ref, g, (y_hi * X_RING + from_x) * 32 + y * 16, 16)
            sems = ref.s_pass.at[g], ref.r_pass.at[g, side]
            for to_core in range(2):
                strip = ref.cross.at[side, to_core, :, columns]
                for to_fsdp in (fsdp, other):
                    send(strip, target, *sems, (to_fsdp, place(1 - y, z, to_core)))

    def along_x(ref, g):
        wait(part(ref, g, 0, 64), ref.r_y.at[g])
        for h in range(2):
            rows = part(ref, g, (h * X_RING + x) * 32 + y * 16, 16)
            for side, (to_fsdp, _) in enumerate(sides):
                send(rows, rows, ref.s_x.at[g], ref.r_x.at[g, side], (to_fsdp, shard))

    def relay(ref, g):
        for side, (to_fsdp, from_x) in enumerate(sides):
            wait(part(ref, g, 0, 32), ref.r_x.at[g, side])
            wait(part(ref, g, 0, 32), ref.r_pass.at[g, side])
            rows = part(ref, g, (side * X_RING + from_x) * 32, 32)
            send(rows, rows, ref.s_x.at[g], ref.r_relay.at[g, side], (to_fsdp, shard))

    def run(ref):
        k = ref.k
        exchange(ref)
        send_weights()
        terms = orthogonalize(ref)
        prepare(ref, terms, 0)
        start_back(ref, 0)
        prepare(ref, terms, 1)
        for source, target, sem in small:
            pltpu.make_async_copy(source, target, sem).wait()
        eta, root = scales()
        wait(ref.weights, ref.r_weights.at[0])
        left_back(ref, 0)
        start_back(ref, 1)
        if k is KEYVAL:
            renew(kv, 0, eta, root)
            along_x(kv, 0)
            pass_on(kv, 0)
            left_back(kv, 1)
            renew(kv, 1, eta, root)
            along_x(kv, 1)
            pass_on(kv, 1)
            relay(kv, 0)
            along_x(q, 0)
            relay(kv, 1)
            along_x(q, 1)
            relay(q, 0)
        else:
            prepare(q, terms, 2)
            along_x(kv, 0)
            renew(q, 0, eta, root)
            along_x(kv, 1)
            left_back(q, 1)
            start_back(q, 2)
            prepare(q, terms, 3)
            pass_on(q, 0)
            along_x(q, 0)
            renew(q, 1, eta, root)
            left_back(q, 2)
            start_back(q, 3)
            relay(kv, 0)
            pass_on(q, 1)
            renew(q, 2, eta, root)
            along_x(q, 1)
            left_back(q, 3)
            renew(q, 3, eta, root)
            relay(kv, 1)
            pass_on(q, 2)
            pass_on(q, 3)
            relay(q, 0)
        along_x(q, 2)
        along_x(q, 3)
        relay(q, 1)
        relay(q, 2)
        relay(q, 3)
        for g in range(len(k.back)):
            wait(part(ref, g, 0, 112), ref.s_y.at[g])
            wait(part(ref, g, 0, 64), ref.s_cross.at[g])
            wait(part(ref, g, 0, 128), ref.s_pass.at[g])
        for g in range(k.chunks):
            most = pl.ds(0, (Z - 1) * k.message)
            wait(ref.out_z.at[g, most, :], ref.s_z.at[g])
        wait(ref.weights.at[0], ref.s_weights.at[0])
        away = kv if ref is q else q
        wait(away.weights.at[pl.ds(0, 2)], away.s_weights.at[0])

    pl.when(core == 0)(lambda: run(q))
    pl.when(core == 1)(lambda: run(kv))

    for ref in both:
        for g in range(len(ref.k.back)):
            wait(part(ref, g, 0, 32), ref.r_relay.at[g, 0])
            wait(part(ref, g, 0, 32), ref.r_relay.at[g, 1])
            wait(part(ref, g, 0, 128), ref.s_x.at[g])


def per_device(
    query_momentum, key_value_momentum, query_blocks, key_value_blocks, clip_flags, logit_max
):
    hbm = pl.BlockSpec(memory_space=pltpu.HBM)
    anywhere = pl.BlockSpec(memory_space=pl.ANY)
    scratch = [
        pltpu.VMEM((1, 32), jnp.int32),
        pltpu.VMEM((1, 32), F32),
        pltpu.SemaphoreType.DMA((2,)),
    ]
    for k in KINDS:
        scratch += list(scratch_of(k).values())
    return pl.pallas_call(
        kernel,
        name="muon",
        out_shape=tuple(pltpu.VMEM((256, k.piece), BF16) for k in KINDS),
        in_specs=[hbm] * 6,
        out_specs=(anywhere, anywhere),
        scratch_shapes=scratch,
        compiler_params=pltpu.CompilerParams(
            collective_id=0, has_side_effects=True, vmem_limit_bytes=60 * 1024 * 1024
        ),
    )(
        query_momentum,
        key_value_momentum,
        query_blocks,
        key_value_blocks,
        clip_flags.reshape(1, 32),
        logit_max.reshape(1, 32),
    )


def solution(mesh):
    placed = (
        P("fsdp", "shard"),
        P("fsdp", "shard"),
        P("fsdp", "shard"),
        P("fsdp", "shard"),
        P("fsdp"),
        P("fsdp"),
    )
    return jax.shard_map(
        per_device,
        mesh=mesh,
        in_specs=placed,
        out_specs=(P(None, "shard"), P(None, "shard")),
        check_vma=False,
    )
```

```python
import functools
import math
from types import SimpleNamespace

import jax
import jax.numpy as jnp
from jax import lax
from jax.experimental import pallas as pl
from jax.experimental.pallas import tpu as pltpu
from jax.sharding import PartitionSpec as P

COEF_A = 3.4445
COEF_B = -4.775
COEF_C = 2.0315
CLIP_TAU = 100.0
LEARNING_RATE = 0.5
DECAY_WEIGHT = 0.1
NS_ITERS = 5
PLAIN = 128

F32 = jnp.float32
BF16 = jnp.bfloat16
Z = 16
LANE = 128
X_RING = 4
MESH = pl.DeviceIdType.MESH


def make_kind(name, rows, rank, chunks, back):
    slabs = rank // LANE
    per_chunk = slabs // chunks
    sources = 4 * rows
    return SimpleNamespace(
        name=name,
        rows=rows,
        rank=rank,
        chunks=chunks,
        slabs=slabs,
        per_chunk=per_chunk,
        sources=sources,
        message=sources * per_chunk,
        size=Z * sources,
        piece=rows * rank,
        strip=rows * per_chunk * LANE,
        span=per_chunk * LANE,
        back=tuple((sum(back[:i]), n) for i, n in enumerate(back)),
    )


UNIT = 512
QUERY = make_kind("q", 3, 1536, 3, (3, 3, 2, 1))
KEYVAL = make_kind("kv", 4, 512, 2, (2, 2))
KINDS = (QUERY, KEYVAL)


def scratch_of(kind):
    g, b = kind.chunks, len(kind.back)
    back_size = Z * 4 * kind.piece // LANE
    dma = pltpu.SemaphoreType.DMA
    return dict(
        raw=pltpu.VMEM((32, kind.piece), F32),
        mom=pltpu.VMEM((g, 32, kind.strip), BF16),
        gather=pltpu.VMEM((g, 4, 16, kind.strip), BF16),
        weights=pltpu.VMEM((4, 16, kind.piece), BF16),
        turn=pltpu.VMEM((Z * kind.message, LANE), F32),
        out_z=pltpu.VMEM((g, Z * kind.message, LANE), BF16),
        in_z=pltpu.VMEM((g, Z * kind.message, LANE), BF16),
        back_out=pltpu.VMEM((back_size, LANE), BF16),
        back_in=pltpu.VMEM((back_size, LANE), BF16),
        matrix=pltpu.VMEM((kind.size, kind.rank), BF16),
        strips=pltpu.VMEM((4, 16, kind.piece), BF16),
        r_raw=dma((1,)),
        cross=pltpu.VMEM((2, 2, 16, kind.piece), BF16),
        s_cross=dma((b,)),
        r_cross=dma((b, 2)),
        s_pass=dma((b,)),
        r_pass=dma((b, 2)),
        s_gather=dma((g,)),
        r_gather=dma((g,)),
        s_weights=dma((1,)),
        r_weights=dma((1,)),
        s_z=dma((g,)),
        r_z=dma((g,)),
        s_back=dma((b,)),
        r_back=dma((b,)),
        s_y=dma((b,)),
        r_y=dma((b,)),
        s_x=dma((b,)),
        r_x=dma((b, 2)),
        r_relay=dma((b, 2)),
    )


NAMES = tuple(scratch_of(QUERY))


def split(value):
    high = value.astype(BF16)
    return high, (value - high.astype(F32)).astype(BF16)


def dot(left, right):
    return jnp.dot(left, right, preferred_element_type=F32)


def products(lefts, right):
    high, low = right
    size = high.shape[0]
    by_high = dot(jnp.concatenate([term for left in lefts for term in left], axis=0), high)
    by_low = dot(jnp.concatenate([left[0] for left in lefts], axis=0), low)
    results = []
    for i in range(len(lefts)):
        first, second = 2 * i * size, (2 * i + 1) * size
        small = by_high[second : second + size] + by_low[i * size : (i + 1) * size]
        results.append(by_high[first : first + size] + small)
    return results


def identity(size):
    first = lax.broadcasted_iota(jnp.int32, (size, size), 0)
    second = lax.broadcasted_iota(jnp.int32, (size, size), 1)
    return first == second


def newton_schulz(gram, size):
    diagonal = identity(size)
    square = jnp.sum(jnp.where(diagonal, gram, 0.0), axis=(0, 1), keepdims=True)
    inverse = 1.0 / (jnp.sqrt(square) + 1e-07)
    a = (gram * inverse) * inverse
    total = None
    for step in range(NS_ITERS):
        a_parts = split(a)
        poly = COEF_B * a + COEF_C * products([a_parts], a_parts)[0]
        poly = jnp.where(diagonal, poly + COEF_A, poly)
        parts = split(poly)
        lefts = [a_parts] if step < NS_ITERS - 1 else []
        if total is not None:
            lefts.append(split(total))
        results = products(lefts, parts)
        total = poly if total is None else results.pop()
        if results:
            a = products([split(results[0])], parts)[0]
    return total * inverse


def kernel(q_mom, kv_mom, q_weights, kv_weights, flags_in, logit_in, q_out, kv_out, *scratch):
    flags, logit, small_sems, *scratch = scratch
    fsdp = lax.axis_index("fsdp")
    shard = lax.axis_index("shard")
    y_hi, x = fsdp // X_RING, fsdp % X_RING
    y, z, core = shard // 32, (shard // 2) % Z, shard % 2
    me = y * 2 + core
    half = len(NAMES)
    q = SimpleNamespace(
        k=QUERY, m=q_mom, w=q_weights, out=q_out, **dict(zip(NAMES, scratch[:half]))
    )
    kv = SimpleNamespace(
        k=KEYVAL, m=kv_mom, w=kv_weights, out=kv_out, **dict(zip(NAMES, scratch[half:]))
    )
    both = (q, kv)

    def place(to_y, to_z, to_core):
        return to_y * 32 + to_z * 2 + to_core

    def send(source, target, s_sem, r_sem, device):
        pltpu.make_async_remote_copy(
            src_ref=source,
            dst_ref=target,
            send_sem=s_sem,
            recv_sem=r_sem,
            device_id=device,
            device_id_type=MESH,
        ).start()

    def keep(source, target, sem):
        pltpu.make_async_copy(source, target, sem).start()

    def wait(ref, sem):
        pltpu.make_async_copy(ref, ref, sem).wait()

    x_right = y_hi * X_RING + (x + 1) % X_RING
    x_left = y_hi * X_RING + (x + X_RING - 1) % X_RING
    other = (1 - y_hi) * X_RING + x

    for ref in both:
        pltpu.make_async_copy(ref.m, ref.raw, ref.r_raw.at[0]).start()
    small = ((flags_in, flags, small_sems.at[0]), (logit_in, logit, small_sems.at[1]))
    for source, target, sem in small:
        pltpu.make_async_copy(source, target, sem).start()
    barrier = pltpu.get_barrier_semaphore()

    def greet(to_fsdp, to_shard):
        pl.semaphore_signal(barrier, inc=1, device_id=(to_fsdp, to_shard), device_id_type=MESH)

    greet(fsdp, place(y, z, 1 - core))
    greet(fsdp, place(1 - y, z, core))
    greet(fsdp, place(1 - y, z, 1 - core))
    for to_y in (y, 1 - y):
        for to_core in (core, 1 - core):
            greet(other, place(to_y, z, to_core))
    greet(x_right, shard)
    greet(x_left, shard)

    def greet_z(step, carry):
        greet(fsdp, place(y, (z + step) % Z, core))
        return carry

    lax.fori_loop(1, Z, greet_z, 0)

    for ref in both:
        k = ref.k
        pltpu.make_async_copy(ref.m, ref.raw, ref.r_raw.at[0]).wait()
        for g in range(k.chunks):
            for r in range(k.rows):
                start = (r * k.slabs + g * k.per_chunk) * LANE
                ref.mom[g, :, r * k.span : (r + 1) * k.span] = ref.raw[
                    :, start : start + k.span
                ].astype(BF16)

    pl.semaphore_wait(barrier, 24)

    def to_group(ref, to_core, source, target, s_sem, r_sem):
        @pl.when(core == to_core)
        def _():
            keep(source(y), target, r_sem)

        @pl.when(core != to_core)
        def _():
            send(source(y), target, s_sem, r_sem, (fsdp, place(y, z, to_core)))

        send(source(1 - y), target, s_sem, r_sem, (fsdp, place(1 - y, z, to_core)))

    def rows16(to_y):
        return pl.ds(pl.multiple_of(to_y * 16, 16), 16)

    def gather(g):
        for to_core, ref in enumerate(both):
            if g < ref.k.chunks:
                to_group(
                    ref,
                    to_core,
                    lambda to_y, ref=ref: ref.mom.at[g, rows16(to_y), :],
                    ref.gather.at[g, me],
                    ref.s_gather.at[g],
                    ref.r_gather.at[g],
                )

    def gathered(own, g):
        for ref in both:
            if g < ref.k.chunks:
                strips = ref.mom.at[g, pl.ds(0, 16), :] if ref is own else ref.mom.at[g]
                wait(strips, ref.s_gather.at[g])

    def send_weights():
        for to_core, ref in enumerate(both):
            to_group(
                ref,
                to_core,
                lambda to_y, ref=ref: ref.w.at[rows16(to_y), :],
                ref.weights.at[me],
                ref.s_weights.at[0],
                ref.r_weights.at[0],
            )

    def z_send(rows, source, target, s_sem, r_sem):
        def one(i, carry):
            far = jnp.where(i % 2 == 1, 8 - (i + 1) // 2, 8 + i // 2)
            to_z = (z + far) % Z
            start = pl.multiple_of(to_z * rows, 16)
            send(
                source.at[pl.ds(start, rows), :],
                target.at[pl.ds(pl.multiple_of(z * rows, 16), rows), :],
                s_sem,
                r_sem,
                (fsdp, place(y, to_z, core)),
            )
            return carry

        lax.fori_loop(0, Z - 1, one, 0)
        here = pl.ds(pl.multiple_of(z * rows, 16), rows)
        keep(source.at[here, :], target.at[here, :], r_sem)

    def every(rows, offset):
        return pl.ds(offset, 16, stride=rows)

    def exchange(ref):
        k = ref.k
        rounds = max(kind.chunks for kind in KINDS)
        gather(0)
        for g in range(rounds):
            gathered(ref, g)
            if g + 1 < rounds:
                gather(g + 1)
            if g >= k.chunks:
                continue
            wait(ref.gather.at[g], ref.r_gather.at[g])
            for s in range(4):
                for r in range(k.rows):
                    for c in range(k.per_chunk):
                        start = (r * k.per_chunk + c) * LANE
                        tile = ref.gather[g, s, :, start : start + LANE]
                        ref.turn[every(k.message, c * k.sources + r * 4 + s), :] = tile.astype(F32)
            ref.out_z[g] = ref.turn[...].astype(BF16)
            z_send(k.message, ref.out_z.at[g], ref.in_z.at[g], ref.s_z.at[g], ref.r_z.at[g])

    def orthogonalize(ref):
        k = ref.k
        gram = None
        for g in range(k.chunks):
            wait(ref.in_z.at[g], ref.r_z.at[g])
            ref.turn[...] = ref.in_z[g].astype(F32)
            for c in range(k.per_chunk):
                column = (g * k.per_chunk + c) * LANE
                for n in range(k.sources):
                    tile = ref.turn[every(k.message, c * k.sources + n), :]
                    ref.matrix[n * 16 : n * 16 + 16, column : column + LANE] = tile.astype(BF16)
            part = ref.matrix[:, g * k.span : (g + 1) * k.span]
            term = lax.dot_general(
                part, part, (((1,), (1,)), ((), ())), preferred_element_type=F32
            )
            gram = term if gram is None else gram + term
        return split(newton_schulz(gram, k.size))

    def prepare(ref, terms, g):
        k = ref.k
        high, low = terms
        first, units = k.back[g]
        for i in range(units):
            row, column = divmod((first + i) * UNIT, k.rank)
            own = slice(row * 64, row * 64 + 64)
            both_terms = jnp.concatenate([high[own], low[own]], axis=0)
            both_terms = dot(both_terms, ref.matrix[:, column : column + UNIT])
            update = both_terms[:64] + both_terms[64:]
            for n in range(4):
                for c in range(4):
                    ref.turn[every(units * 16, i * 16 + n * 4 + c), :] = update[
                        n * 16 : n * 16 + 16, c * LANE : (c + 1) * LANE
                    ]
        ref.back_out[back_span(first, units), :] = ref.turn[: Z * units * 16].astype(BF16)

    def start_back(ref, g):
        first, units = ref.k.back[g]
        span = back_span(first, units)
        sems = ref.s_back.at[g], ref.r_back.at[g]
        z_send(units * 16, ref.back_out.at[span, :], ref.back_in.at[span, :], *sems)

    def left_back(ref, g):
        units = ref.k.back[g][1]
        wait(ref.back_out.at[pl.ds(0, (Z - 1) * 16 * units), :], ref.s_back.at[g])

    def back_span(first, units):
        return pl.ds(Z * 16 * first, Z * 16 * units)

    sides = (
        (x_right, lax.rem(x + X_RING - 1, X_RING)),
        (x_left, lax.rem(x + 1, X_RING)),
    )

    def scales():
        ratio = jnp.minimum(1.0, CLIP_TAU / logit[...])
        eta_row = jnp.where(flags[...] > 0, ratio, 1.0)
        spread = jnp.where(identity(32), jnp.broadcast_to(eta_row, (32, 32)), 0.0)
        column = jnp.sum(spread, axis=1, keepdims=True)
        eta = jnp.where(y == 0, column[:16], column[16:])
        return jnp.broadcast_to(eta, (16, LANE)), jnp.broadcast_to(jnp.sqrt(eta), (16, LANE))

    def part(ref, g, start, count):
        rows = pl.ds(pl.multiple_of(start, 16), count)
        return ref.out.at[rows, chunk_columns(ref, g)]

    def chunk_columns(ref, g):
        first, units = ref.k.back[g]
        return slice(first * UNIT, (first + units) * UNIT)

    def renew(ref, g, eta, root):
        k = ref.k
        first, units = k.back[g]
        span = back_span(first, units)
        wait(ref.back_in.at[span, :], ref.r_back.at[g])
        ref.turn[: Z * units * 16] = ref.back_in[span, :].astype(F32)
        tail = eta if k is QUERY else jnp.ones_like(eta)
        for i in range(units):
            for s in range(4):
                row = (first + i) * UNIT // k.rank
                row = ((s // 2) * 32 + z * 2 + s % 2) * k.rows + row
                scale = jnp.where(row < PLAIN, root, tail)
                for c in range(4):
                    update = ref.turn[every(units * 16, i * 16 + s * 4 + c), :]
                    column = (first + i) * UNIT + c * LANE
                    old = ref.weights[s, :, column : column + LANE].astype(F32)
                    fresh = scale * (
                        old * (1.0 - LEARNING_RATE * DECAY_WEIGHT)
                        - LEARNING_RATE * 0.2 * math.sqrt(k.rank) * update
                    )
                    ref.strips[s, :, column : column + LANE] = fresh.astype(BF16)
        columns = chunk_columns(ref, g)
        mine = part(ref, g, fsdp * 32 + y * 16, 16)
        pair = ref.strips.at[pl.ds(pl.multiple_of((1 - y) * 2, 2), 2), :, columns]
        for side, (to_fsdp, _) in enumerate(sides):
            target = ref.cross.at[side, :, :, columns]
            send(pair, target, ref.s_cross.at[g], ref.r_cross.at[g, side], (to_fsdp, shard))
        sems = ref.s_y.at[g], ref.r_y.at[g]
        for to_core in (core, 1 - core):
            strip = ref.strips.at[y * 2 + to_core, :, columns]
            send(strip, mine, *sems, (other, place(y, z, to_core)))
            strip = ref.strips.at[(1 - y) * 2 + to_core, :, columns]
            send(strip, mine, *sems, (fsdp, place(1 - y, z, to_core)))
            send(strip, mine, *sems, (other, place(1 - y, z, to_core)))
        strip = ref.strips.at[y * 2 + 1 - core, :, columns]
        send(strip, mine, *sems, (fsdp, place(y, z, 1 - core)))
        keep(ref.strips.at[me, :, columns], mine, ref.r_y.at[g])

    def pass_on(ref, g):
        columns = chunk_columns(ref, g)
        for side, (_, from_x) in enumerate(sides):
            landed = ref.cross.at[side, :, :, columns]
            wait(landed, ref.r_cross.at[g, side])
            target = part(ref, g, (y_hi * X_RING + from_x) * 32 + y * 16, 16)
            sems = ref.s_pass.at[g], ref.r_pass.at[g, side]
            for to_core in range(2):
                strip = ref.cross.at[side, to_core, :, columns]
                for to_fsdp in (fsdp, other):
                    send(strip, target, *sems, (to_fsdp, place(1 - y, z, to_core)))

    def along_x(ref, g):
        wait(part(ref, g, 0, 64), ref.r_y.at[g])
        for h in range(2):
            rows = part(ref, g, (h * X_RING + x) * 32 + y * 16, 16)
            for side, (to_fsdp, _) in enumerate(sides):
                send(rows, rows, ref.s_x.at[g], ref.r_x.at[g, side], (to_fsdp, shard))

    def relay(ref, g):
        for side, (to_fsdp, from_x) in enumerate(sides):
            wait(part(ref, g, 0, 32), ref.r_x.at[g, side])
            wait(part(ref, g, 0, 32), ref.r_pass.at[g, side])
            rows = part(ref, g, (side * X_RING + from_x) * 32, 32)
            send(rows, rows, ref.s_x.at[g], ref.r_relay.at[g, side], (to_fsdp, shard))

    def run(ref):
        k = ref.k
        exchange(ref)
        send_weights()
        terms = orthogonalize(ref)
        prepare(ref, terms, 0)
        start_back(ref, 0)
        prepare(ref, terms, 1)
        for source, target, sem in small:
            pltpu.make_async_copy(source, target, sem).wait()
        eta, root = scales()
        wait(ref.weights, ref.r_weights.at[0])
        left_back(ref, 0)
        start_back(ref, 1)
        if k is KEYVAL:
            renew(kv, 0, eta, root)
            along_x(kv, 0)
            pass_on(kv, 0)
            left_back(kv, 1)
            renew(kv, 1, eta, root)
            along_x(kv, 1)
            pass_on(kv, 1)
            relay(kv, 0)
            along_x(q, 0)
            relay(kv, 1)
            along_x(q, 1)
            relay(q, 0)
        else:
            prepare(q, terms, 2)
            along_x(kv, 0)
            renew(q, 0, eta, root)
            along_x(kv, 1)
            relay(kv, 0)
            left_back(q, 1)
            start_back(q, 2)
            pass_on(q, 0)
            along_x(q, 0)
            prepare(q, terms, 3)
            renew(q, 1, eta, root)
            relay(kv, 1)
            left_back(q, 2)
            start_back(q, 3)
            pass_on(q, 1)
            renew(q, 2, eta, root)
            along_x(q, 1)
            renew(q, 3, eta, root)
            relay(q, 0)
            pass_on(q, 2)
            pass_on(q, 3)
        along_x(q, 2)
        along_x(q, 3)
        relay(q, 1)
        relay(q, 2)
        relay(q, 3)
        if k is QUERY:
            left_back(q, 3)
        for g in range(len(k.back)):
            wait(part(ref, g, 0, 112), ref.s_y.at[g])
            wait(part(ref, g, 0, 64), ref.s_cross.at[g])
            wait(part(ref, g, 0, 128), ref.s_pass.at[g])
        for g in range(k.chunks):
            most = pl.ds(0, (Z - 1) * k.message)
            wait(ref.out_z.at[g, most, :], ref.s_z.at[g])
        wait(ref.weights.at[0], ref.s_weights.at[0])
        away = kv if ref is q else q
        wait(away.weights.at[pl.ds(0, 2)], away.s_weights.at[0])

    pl.when(core == 0)(lambda: run(q))
    pl.when(core == 1)(lambda: run(kv))

    for ref in both:
        for g in range(len(ref.k.back)):
            wait(part(ref, g, 0, 32), ref.r_relay.at[g, 0])
            wait(part(ref, g, 0, 32), ref.r_relay.at[g, 1])
            wait(part(ref, g, 0, 128), ref.s_x.at[g])


def per_device(
    query_momentum, key_value_momentum, query_blocks, key_value_blocks, clip_flags, logit_max
):
    hbm = pl.BlockSpec(memory_space=pltpu.HBM)
    anywhere = pl.BlockSpec(memory_space=pl.ANY)
    scratch = [
        pltpu.VMEM((1, 32), jnp.int32),
        pltpu.VMEM((1, 32), F32),
        pltpu.SemaphoreType.DMA((2,)),
    ]
    for k in KINDS:
        scratch += list(scratch_of(k).values())
    return pl.pallas_call(
        kernel,
        name="muon",
        out_shape=tuple(pltpu.VMEM((256, k.piece), BF16) for k in KINDS),
        in_specs=[hbm] * 6,
        out_specs=(anywhere, anywhere),
        scratch_shapes=scratch,
        compiler_params=pltpu.CompilerParams(
            collective_id=0, has_side_effects=True, vmem_limit_bytes=60 * 1024 * 1024
        ),
    )(
        query_momentum,
        key_value_momentum,
        query_blocks,
        key_value_blocks,
        clip_flags.reshape(1, 32),
        logit_max.reshape(1, 32),
    )


def solution(mesh):
    placed = (
        P("fsdp", "shard"),
        P("fsdp", "shard"),
        P("fsdp", "shard"),
        P("fsdp", "shard"),
        P("fsdp"),
        P("fsdp"),
    )
    return jax.shard_map(
        per_device,
        mesh=mesh,
        in_specs=placed,
        out_specs=(P(None, "shard"), P(None, "shard")),
        check_vma=False,
    )
```

```python
import functools
import math
from types import SimpleNamespace

import jax
import jax.numpy as jnp
from jax import lax
from jax.experimental import pallas as pl
from jax.experimental.pallas import tpu as pltpu
from jax.sharding import PartitionSpec as P

COEF_A = 3.4445
COEF_B = -4.775
COEF_C = 2.0315
CLIP_TAU = 100.0
LEARNING_RATE = 0.5
DECAY_WEIGHT = 0.1
NS_ITERS = 5
PLAIN = 128

F32 = jnp.float32
BF16 = jnp.bfloat16
Z = 16
LANE = 128
X_RING = 4
MESH = pl.DeviceIdType.MESH


def make_kind(name, rows, rank, chunks, back):
    slabs = rank // LANE
    per_chunk = slabs // chunks
    sources = 4 * rows
    return SimpleNamespace(
        name=name,
        rows=rows,
        rank=rank,
        chunks=chunks,
        slabs=slabs,
        per_chunk=per_chunk,
        sources=sources,
        message=sources * per_chunk,
        size=Z * sources,
        piece=rows * rank,
        strip=rows * per_chunk * LANE,
        span=per_chunk * LANE,
        back=tuple((sum(back[:i]), n) for i, n in enumerate(back)),
    )


UNIT = 512
QUERY = make_kind("q", 3, 1536, 3, (3, 3, 2, 1))
KEYVAL = make_kind("kv", 4, 512, 2, (2, 2))
KINDS = (QUERY, KEYVAL)


def scratch_of(kind):
    g, b = kind.chunks, len(kind.back)
    back_size = Z * 4 * kind.piece // LANE
    dma = pltpu.SemaphoreType.DMA
    return dict(
        raw=pltpu.VMEM((32, kind.piece), F32),
        mom=pltpu.VMEM((g, 32, kind.strip), BF16),
        gather=pltpu.VMEM((g, 4, 16, kind.strip), BF16),
        weights=pltpu.VMEM((4, 16, kind.piece), BF16),
        turn=pltpu.VMEM((Z * kind.message, LANE), F32),
        out_z=pltpu.VMEM((g, Z * kind.message, LANE), BF16),
        in_z=pltpu.VMEM((g, Z * kind.message, LANE), BF16),
        back_out=pltpu.VMEM((back_size, LANE), BF16),
        back_in=pltpu.VMEM((back_size, LANE), BF16),
        matrix=pltpu.VMEM((kind.size, kind.rank), BF16),
        strips=pltpu.VMEM((4, 16, kind.piece), BF16),
        r_raw=dma((1,)),
        cross=pltpu.VMEM((2, 2, 16, kind.piece), BF16),
        s_cross=dma((b,)),
        r_cross=dma((b, 2)),
        s_pass=dma((b,)),
        r_pass=dma((b, 2)),
        s_gather=dma((g,)),
        r_gather=dma((g,)),
        s_weights=dma((1,)),
        r_weights=dma((1,)),
        s_z=dma((g,)),
        r_z=dma((g,)),
        s_back=dma((b,)),
        r_back=dma((b,)),
        s_y=dma((b,)),
        r_y=dma((b,)),
        s_x=dma((b,)),
        r_x=dma((b, 2)),
        r_relay=dma((b, 2)),
    )


NAMES = tuple(scratch_of(QUERY))


def split(value):
    high = value.astype(BF16)
    return high, (value - high.astype(F32)).astype(BF16)


def dot(left, right):
    return jnp.dot(left, right, preferred_element_type=F32)


def products(lefts, right):
    high, low = right
    size = high.shape[0]
    by_high = dot(jnp.concatenate([term for left in lefts for term in left], axis=0), high)
    by_low = dot(jnp.concatenate([left[0] for left in lefts], axis=0), low)
    results = []
    for i in range(len(lefts)):
        first, second = 2 * i * size, (2 * i + 1) * size
        small = by_high[second : second + size] + by_low[i * size : (i + 1) * size]
        results.append(by_high[first : first + size] + small)
    return results


def identity(size):
    first = lax.broadcasted_iota(jnp.int32, (size, size), 0)
    second = lax.broadcasted_iota(jnp.int32, (size, size), 1)
    return first == second


def newton_schulz(gram, size):
    diagonal = identity(size)
    square = jnp.sum(jnp.where(diagonal, gram, 0.0), axis=(0, 1), keepdims=True)
    inverse = 1.0 / (jnp.sqrt(square) + 1e-07)
    a = (gram * inverse) * inverse
    total = None
    for step in range(NS_ITERS):
        a_parts = split(a)
        poly = COEF_B * a + COEF_C * products([a_parts], a_parts)[0]
        poly = jnp.where(diagonal, poly + COEF_A, poly)
        parts = split(poly)
        lefts = [a_parts] if step < NS_ITERS - 1 else []
        if total is not None:
            lefts.append(split(total))
        results = products(lefts, parts)
        total = poly if total is None else results.pop()
        if results:
            a = products([split(results[0])], parts)[0]
    return total * inverse


def kernel(q_mom, kv_mom, q_weights, kv_weights, flags_in, logit_in, q_out, kv_out, *scratch):
    flags, logit, small_sems, *scratch = scratch
    fsdp = lax.axis_index("fsdp")
    shard = lax.axis_index("shard")
    y_hi, x = fsdp // X_RING, fsdp % X_RING
    y, z, core = shard // 32, (shard // 2) % Z, shard % 2
    me = y * 2 + core
    half = len(NAMES)
    q = SimpleNamespace(
        k=QUERY, m=q_mom, w=q_weights, out=q_out, **dict(zip(NAMES, scratch[:half]))
    )
    kv = SimpleNamespace(
        k=KEYVAL, m=kv_mom, w=kv_weights, out=kv_out, **dict(zip(NAMES, scratch[half:]))
    )
    both = (q, kv)

    def place(to_y, to_z, to_core):
        return to_y * 32 + to_z * 2 + to_core

    def send(source, target, s_sem, r_sem, device):
        pltpu.make_async_remote_copy(
            src_ref=source,
            dst_ref=target,
            send_sem=s_sem,
            recv_sem=r_sem,
            device_id=device,
            device_id_type=MESH,
        ).start()

    def keep(source, target, sem):
        pltpu.make_async_copy(source, target, sem).start()

    def wait(ref, sem):
        pltpu.make_async_copy(ref, ref, sem).wait()

    x_right = y_hi * X_RING + (x + 1) % X_RING
    x_left = y_hi * X_RING + (x + X_RING - 1) % X_RING
    other = (1 - y_hi) * X_RING + x

    for ref in both:
        pltpu.make_async_copy(ref.m, ref.raw, ref.r_raw.at[0]).start()
    small = ((flags_in, flags, small_sems.at[0]), (logit_in, logit, small_sems.at[1]))
    for source, target, sem in small:
        pltpu.make_async_copy(source, target, sem).start()
    barrier = pltpu.get_barrier_semaphore()

    def greet(to_fsdp, to_shard):
        pl.semaphore_signal(barrier, inc=1, device_id=(to_fsdp, to_shard), device_id_type=MESH)

    greet(fsdp, place(y, z, 1 - core))
    greet(fsdp, place(1 - y, z, core))
    greet(fsdp, place(1 - y, z, 1 - core))
    for to_y in (y, 1 - y):
        for to_core in (core, 1 - core):
            greet(other, place(to_y, z, to_core))
    greet(x_right, shard)
    greet(x_left, shard)

    def greet_z(step, carry):
        greet(fsdp, place(y, (z + step) % Z, core))
        return carry

    lax.fori_loop(1, Z, greet_z, 0)

    for ref in both:
        k = ref.k
        pltpu.make_async_copy(ref.m, ref.raw, ref.r_raw.at[0]).wait()
        for g in range(k.chunks):
            for r in range(k.rows):
                start = (r * k.slabs + g * k.per_chunk) * LANE
                ref.mom[g, :, r * k.span : (r + 1) * k.span] = ref.raw[
                    :, start : start + k.span
                ].astype(BF16)

    pl.semaphore_wait(barrier, 24)

    def to_group(ref, to_core, source, target, s_sem, r_sem):
        @pl.when(core == to_core)
        def _():
            keep(source(y), target, r_sem)

        @pl.when(core != to_core)
        def _():
            send(source(y), target, s_sem, r_sem, (fsdp, place(y, z, to_core)))

        send(source(1 - y), target, s_sem, r_sem, (fsdp, place(1 - y, z, to_core)))

    def rows16(to_y):
        return pl.ds(pl.multiple_of(to_y * 16, 16), 16)

    def gather(g):
        for to_core, ref in enumerate(both):
            if g < ref.k.chunks:
                to_group(
                    ref,
                    to_core,
                    lambda to_y, ref=ref: ref.mom.at[g, rows16(to_y), :],
                    ref.gather.at[g, me],
                    ref.s_gather.at[g],
                    ref.r_gather.at[g],
                )

    def gathered(own, g):
        for ref in both:
            if g < ref.k.chunks:
                strips = ref.mom.at[g, pl.ds(0, 16), :] if ref is own else ref.mom.at[g]
                wait(strips, ref.s_gather.at[g])

    def send_weights():
        for to_core, ref in enumerate(both):
            to_group(
                ref,
                to_core,
                lambda to_y, ref=ref: ref.w.at[rows16(to_y), :],
                ref.weights.at[me],
                ref.s_weights.at[0],
                ref.r_weights.at[0],
            )

    def z_send(rows, source, target, s_sem, r_sem):
        def one(i, carry):
            far = jnp.where(i % 2 == 1, 8 - (i + 1) // 2, 8 + i // 2)
            to_z = (z + far) % Z
            start = pl.multiple_of(to_z * rows, 16)
            send(
                source.at[pl.ds(start, rows), :],
                target.at[pl.ds(pl.multiple_of(z * rows, 16), rows), :],
                s_sem,
                r_sem,
                (fsdp, place(y, to_z, core)),
            )
            return carry

        lax.fori_loop(0, Z - 1, one, 0)
        here = pl.ds(pl.multiple_of(z * rows, 16), rows)
        keep(source.at[here, :], target.at[here, :], r_sem)

    def every(rows, offset):
        return pl.ds(offset, 16, stride=rows)

    def exchange(ref):
        k = ref.k
        rounds = max(kind.chunks for kind in KINDS)
        gather(0)
        for g in range(rounds):
            gathered(ref, g)
            if g + 1 < rounds:
                gather(g + 1)
            if g >= k.chunks:
                continue
            wait(ref.gather.at[g], ref.r_gather.at[g])
            for s in range(4):
                for r in range(k.rows):
                    for c in range(k.per_chunk):
                        start = (r * k.per_chunk + c) * LANE
                        tile = ref.gather[g, s, :, start : start + LANE]
                        ref.turn[every(k.message, c * k.sources + r * 4 + s), :] = tile.astype(F32)
            ref.out_z[g] = ref.turn[...].astype(BF16)
            z_send(k.message, ref.out_z.at[g], ref.in_z.at[g], ref.s_z.at[g], ref.r_z.at[g])

    def orthogonalize(ref):
        k = ref.k
        gram = None
        for g in range(k.chunks):
            wait(ref.in_z.at[g], ref.r_z.at[g])
            ref.turn[...] = ref.in_z[g].astype(F32)
            for c in range(k.per_chunk):
                column = (g * k.per_chunk + c) * LANE
                for n in range(k.sources):
                    tile = ref.turn[every(k.message, c * k.sources + n), :]
                    ref.matrix[n * 16 : n * 16 + 16, column : column + LANE] = tile.astype(BF16)
            part = ref.matrix[:, g * k.span : (g + 1) * k.span]
            term = lax.dot_general(
                part, part, (((1,), (1,)), ((), ())), preferred_element_type=F32
            )
            gram = term if gram is None else gram + term
        return split(newton_schulz(gram, k.size))

    def prepare(ref, terms, g):
        k = ref.k
        high, low = terms
        first, units = k.back[g]
        for i in range(units):
            row, column = divmod((first + i) * UNIT, k.rank)
            own = slice(row * 64, row * 64 + 64)
            both_terms = jnp.concatenate([high[own], low[own]], axis=0)
            both_terms = dot(both_terms, ref.matrix[:, column : column + UNIT])
            update = both_terms[:64] + both_terms[64:]
            for n in range(4):
                for c in range(4):
                    ref.turn[every(units * 16, i * 16 + n * 4 + c), :] = update[
                        n * 16 : n * 16 + 16, c * LANE : (c + 1) * LANE
                    ]
        ref.back_out[back_span(first, units), :] = ref.turn[: Z * units * 16].astype(BF16)

    def start_back(ref, g):
        first, units = ref.k.back[g]
        span = back_span(first, units)
        sems = ref.s_back.at[g], ref.r_back.at[g]
        z_send(units * 16, ref.back_out.at[span, :], ref.back_in.at[span, :], *sems)

    def left_back(ref, g):
        units = ref.k.back[g][1]
        wait(ref.back_out.at[pl.ds(0, (Z - 1) * 16 * units), :], ref.s_back.at[g])

    def back_span(first, units):
        return pl.ds(Z * 16 * first, Z * 16 * units)

    sides = (
        (x_right, lax.rem(x + X_RING - 1, X_RING)),
        (x_left, lax.rem(x + 1, X_RING)),
    )

    def scales():
        ratio = jnp.minimum(1.0, CLIP_TAU / logit[...])
        eta_row = jnp.where(flags[...] > 0, ratio, 1.0)
        spread = jnp.where(identity(32), jnp.broadcast_to(eta_row, (32, 32)), 0.0)
        column = jnp.sum(spread, axis=1, keepdims=True)
        eta = jnp.where(y == 0, column[:16], column[16:])
        return jnp.broadcast_to(eta, (16, LANE)), jnp.broadcast_to(jnp.sqrt(eta), (16, LANE))

    def part(ref, g, start, count):
        rows = pl.ds(pl.multiple_of(start, 16), count)
        return ref.out.at[rows, chunk_columns(ref, g)]

    def chunk_columns(ref, g):
        first, units = ref.k.back[g]
        return slice(first * UNIT, (first + units) * UNIT)

    def renew(ref, g, eta, root):
        k = ref.k
        first, units = k.back[g]
        span = back_span(first, units)
        wait(ref.back_in.at[span, :], ref.r_back.at[g])
        ref.turn[: Z * units * 16] = ref.back_in[span, :].astype(F32)
        tail = eta if k is QUERY else jnp.ones_like(eta)
        for i in range(units):
            for s in range(4):
                row = (first + i) * UNIT // k.rank
                row = ((s // 2) * 32 + z * 2 + s % 2) * k.rows + row
                scale = jnp.where(row < PLAIN, root, tail)
                for c in range(4):
                    update = ref.turn[every(units * 16, i * 16 + s * 4 + c), :]
                    column = (first + i) * UNIT + c * LANE
                    old = ref.weights[s, :, column : column + LANE].astype(F32)
                    fresh = scale * (
                        old * (1.0 - LEARNING_RATE * DECAY_WEIGHT)
                        - LEARNING_RATE * 0.2 * math.sqrt(k.rank) * update
                    )
                    ref.strips[s, :, column : column + LANE] = fresh.astype(BF16)
        columns = chunk_columns(ref, g)
        mine = part(ref, g, fsdp * 32 + y * 16, 16)
        pair = ref.strips.at[pl.ds(pl.multiple_of((1 - y) * 2, 2), 2), :, columns]
        for side, (to_fsdp, _) in enumerate(sides):
            target = ref.cross.at[side, :, :, columns]
            send(pair, target, ref.s_cross.at[g], ref.r_cross.at[g, side], (to_fsdp, shard))
        sems = ref.s_y.at[g], ref.r_y.at[g]
        for to_core in (core, 1 - core):
            strip = ref.strips.at[y * 2 + to_core, :, columns]
            send(strip, mine, *sems, (other, place(y, z, to_core)))
            strip = ref.strips.at[(1 - y) * 2 + to_core, :, columns]
            send(strip, mine, *sems, (fsdp, place(1 - y, z, to_core)))
            send(strip, mine, *sems, (other, place(1 - y, z, to_core)))
        strip = ref.strips.at[y * 2 + 1 - core, :, columns]
        send(strip, mine, *sems, (fsdp, place(y, z, 1 - core)))
        keep(ref.strips.at[me, :, columns], mine, ref.r_y.at[g])

    def pass_on(ref, g):
        columns = chunk_columns(ref, g)
        for side, (_, from_x) in enumerate(sides):
            landed = ref.cross.at[side, :, :, columns]
            wait(landed, ref.r_cross.at[g, side])
            target = part(ref, g, (y_hi * X_RING + from_x) * 32 + y * 16, 16)
            sems = ref.s_pass.at[g], ref.r_pass.at[g, side]
            for to_core in range(2):
                strip = ref.cross.at[side, to_core, :, columns]
                for to_fsdp in (fsdp, other):
                    send(strip, target, *sems, (to_fsdp, place(1 - y, z, to_core)))

    def along_x(ref, g):
        wait(part(ref, g, 0, 64), ref.r_y.at[g])
        for h in range(2):
            rows = part(ref, g, (h * X_RING + x) * 32 + y * 16, 16)
            for side, (to_fsdp, _) in enumerate(sides):
                send(rows, rows, ref.s_x.at[g], ref.r_x.at[g, side], (to_fsdp, shard))

    def relay(ref, g):
        for side, (to_fsdp, from_x) in enumerate(sides):
            wait(part(ref, g, 0, 32), ref.r_x.at[g, side])
            wait(part(ref, g, 0, 32), ref.r_pass.at[g, side])
            rows = part(ref, g, (side * X_RING + from_x) * 32, 32)
            send(rows, rows, ref.s_x.at[g], ref.r_relay.at[g, side], (to_fsdp, shard))

    def run(ref):
        k = ref.k
        exchange(ref)
        send_weights()
        terms = orthogonalize(ref)
        prepare(ref, terms, 0)
        start_back(ref, 0)
        prepare(ref, terms, 1)
        for source, target, sem in small:
            pltpu.make_async_copy(source, target, sem).wait()
        eta, root = scales()
        wait(ref.weights, ref.r_weights.at[0])
        left_back(ref, 0)
        start_back(ref, 1)
        if k is KEYVAL:
            renew(kv, 0, eta, root)
            pass_on(kv, 0)
            along_x(kv, 0)
            renew(kv, 1, eta, root)
            pass_on(kv, 1)
            along_x(kv, 1)
            relay(kv, 0)
            along_x(q, 0)
            relay(kv, 1)
            along_x(q, 1)
            relay(q, 0)
        else:
            prepare(q, terms, 2)
            prepare(q, terms, 3)
            along_x(kv, 0)
            renew(q, 0, eta, root)
            along_x(kv, 1)
            relay(kv, 0)
            left_back(q, 1)
            start_back(q, 2)
            start_back(q, 3)
            pass_on(q, 0)
            along_x(q, 0)
            renew(q, 1, eta, root)
            relay(kv, 1)
            pass_on(q, 1)
            renew(q, 2, eta, root)
            along_x(q, 1)
            renew(q, 3, eta, root)
            relay(q, 0)
            pass_on(q, 2)
            pass_on(q, 3)
        along_x(q, 2)
        along_x(q, 3)
        relay(q, 1)
        relay(q, 2)
        relay(q, 3)
        for g in range(2 if k is QUERY else 1, len(k.back)):
            left_back(ref, g)
        for g in range(len(k.back)):
            wait(part(ref, g, 0, 112), ref.s_y.at[g])
            wait(part(ref, g, 0, 64), ref.s_cross.at[g])
            wait(part(ref, g, 0, 128), ref.s_pass.at[g])
        for g in range(k.chunks):
            most = pl.ds(0, (Z - 1) * k.message)
            wait(ref.out_z.at[g, most, :], ref.s_z.at[g])
        wait(ref.weights.at[0], ref.s_weights.at[0])
        away = kv if ref is q else q
        wait(away.weights.at[pl.ds(0, 2)], away.s_weights.at[0])

    pl.when(core == 0)(lambda: run(q))
    pl.when(core == 1)(lambda: run(kv))

    for ref in both:
        for g in range(len(ref.k.back)):
            wait(part(ref, g, 0, 32), ref.r_relay.at[g, 0])
            wait(part(ref, g, 0, 32), ref.r_relay.at[g, 1])
            wait(part(ref, g, 0, 128), ref.s_x.at[g])


def per_device(
    query_momentum, key_value_momentum, query_blocks, key_value_blocks, clip_flags, logit_max
):
    hbm = pl.BlockSpec(memory_space=pltpu.HBM)
    anywhere = pl.BlockSpec(memory_space=pl.ANY)
    scratch = [
        pltpu.VMEM((1, 32), jnp.int32),
        pltpu.VMEM((1, 32), F32),
        pltpu.SemaphoreType.DMA((2,)),
    ]
    for k in KINDS:
        scratch += list(scratch_of(k).values())
    return pl.pallas_call(
        kernel,
        name="muon",
        out_shape=tuple(pltpu.VMEM((256, k.piece), BF16) for k in KINDS),
        in_specs=[hbm] * 6,
        out_specs=(anywhere, anywhere),
        scratch_shapes=scratch,
        compiler_params=pltpu.CompilerParams(
            collective_id=0, has_side_effects=True, vmem_limit_bytes=60 * 1024 * 1024
        ),
    )(
        query_momentum,
        key_value_momentum,
        query_blocks,
        key_value_blocks,
        clip_flags.reshape(1, 32),
        logit_max.reshape(1, 32),
    )


def solution(mesh):
    placed = (
        P("fsdp", "shard"),
        P("fsdp", "shard"),
        P("fsdp", "shard"),
        P("fsdp", "shard"),
        P("fsdp"),
        P("fsdp"),
    )
    return jax.shard_map(
        per_device,
        mesh=mesh,
        in_specs=placed,
        out_specs=(P(None, "shard"), P(None, "shard")),
        check_vma=False,
    )
```

```python
import functools
import math
from types import SimpleNamespace

import jax
import jax.numpy as jnp
from jax import lax
from jax.experimental import pallas as pl
from jax.experimental.pallas import tpu as pltpu
from jax.sharding import PartitionSpec as P

COEF_A = 3.4445
COEF_B = -4.775
COEF_C = 2.0315
CLIP_TAU = 100.0
LEARNING_RATE = 0.5
DECAY_WEIGHT = 0.1
NS_ITERS = 5
PLAIN = 128

F32 = jnp.float32
BF16 = jnp.bfloat16
Z = 16
LANE = 128
X_RING = 4
MESH = pl.DeviceIdType.MESH


def make_kind(name, rows, rank, chunks, back):
    slabs = rank // LANE
    per_chunk = slabs // chunks
    sources = 4 * rows
    return SimpleNamespace(
        name=name,
        rows=rows,
        rank=rank,
        chunks=chunks,
        slabs=slabs,
        per_chunk=per_chunk,
        sources=sources,
        message=sources * per_chunk,
        size=Z * sources,
        piece=rows * rank,
        strip=rows * per_chunk * LANE,
        span=per_chunk * LANE,
        back=tuple((sum(back[:i]), n) for i, n in enumerate(back)),
    )


UNIT = 512
QUERY = make_kind("q", 3, 1536, 3, (3, 3, 2, 1))
KEYVAL = make_kind("kv", 4, 512, 2, (2, 2))
KINDS = (QUERY, KEYVAL)


def scratch_of(kind):
    g, b = kind.chunks, len(kind.back)
    back_size = Z * 4 * kind.piece // LANE
    dma = pltpu.SemaphoreType.DMA
    return dict(
        raw=pltpu.VMEM((32, kind.piece), F32),
        mom=pltpu.VMEM((g, 32, kind.strip), BF16),
        gather=pltpu.VMEM((g, 4, 16, kind.strip), BF16),
        weights=pltpu.VMEM((4, 16, kind.piece), BF16),
        turn=pltpu.VMEM((Z * kind.message, LANE), F32),
        out_z=pltpu.VMEM((g, Z * kind.message, LANE), BF16),
        in_z=pltpu.VMEM((g, Z * kind.message, LANE), BF16),
        back_out=pltpu.VMEM((back_size, LANE), BF16),
        back_in=pltpu.VMEM((back_size, LANE), BF16),
        matrix=pltpu.VMEM((kind.size, kind.rank), BF16),
        strips=pltpu.VMEM((4, 16, kind.piece), BF16),
        r_raw=dma((1,)),
        cross=pltpu.VMEM((2, 2, 16, kind.piece), BF16),
        s_cross=dma((b,)),
        r_cross=dma((b, 2)),
        s_pass=dma((b,)),
        r_pass=dma((b, 2)),
        s_gather=dma((g,)),
        r_gather=dma((g,)),
        s_weights=dma((1,)),
        r_weights=dma((1,)),
        s_z=dma((g,)),
        r_z=dma((g,)),
        s_back=dma((b,)),
        r_back=dma((b,)),
        s_y=dma((b,)),
        r_y=dma((b,)),
        s_x=dma((b,)),
        r_x=dma((b, 2)),
        r_relay=dma((b, 2)),
    )


NAMES = tuple(scratch_of(QUERY))


def split(value):
    high = value.astype(BF16)
    return high, (value - high.astype(F32)).astype(BF16)


def dot(left, right):
    return jnp.dot(left, right, preferred_element_type=F32)


def product(left, right):
    return dot(left[0], right[0]) + (dot(left[0], right[1]) + dot(left[1], right[0]))


def identity(size):
    first = lax.broadcasted_iota(jnp.int32, (size, size), 0)
    second = lax.broadcasted_iota(jnp.int32, (size, size), 1)
    return first == second


def newton_schulz(gram, size):
    diagonal = identity(size)
    square = jnp.sum(jnp.where(diagonal, gram, 0.0), axis=(0, 1), keepdims=True)
    inverse = 1.0 / (jnp.sqrt(square) + 1e-07)
    a = (gram * inverse) * inverse
    total = None
    for step in range(NS_ITERS):
        a_parts = split(a)
        poly = COEF_B * a + COEF_C * product(a_parts, a_parts)
        poly = jnp.where(diagonal, poly + COEF_A, poly)
        parts = split(poly)
        total = poly if total is None else product(parts, split(total))
        if step < NS_ITERS - 1:
            a = product(parts, split(product(parts, a_parts)))
    return total * inverse


def kernel(q_mom, kv_mom, q_weights, kv_weights, flags_in, logit_in, q_out, kv_out, *scratch):
    flags, logit, small_sems, *scratch = scratch
    fsdp = lax.axis_index("fsdp")
    shard = lax.axis_index("shard")
    y_hi, x = fsdp // X_RING, fsdp % X_RING
    y, z, core = shard // 32, (shard // 2) % Z, shard % 2
    me = y * 2 + core
    half = len(NAMES)
    q = SimpleNamespace(
        k=QUERY, m=q_mom, w=q_weights, out=q_out, **dict(zip(NAMES, scratch[:half]))
    )
    kv = SimpleNamespace(
        k=KEYVAL, m=kv_mom, w=kv_weights, out=kv_out, **dict(zip(NAMES, scratch[half:]))
    )
    both = (q, kv)

    def place(to_y, to_z, to_core):
        return to_y * 32 + to_z * 2 + to_core

    def send(source, target, s_sem, r_sem, device):
        pltpu.make_async_remote_copy(
            src_ref=source,
            dst_ref=target,
            send_sem=s_sem,
            recv_sem=r_sem,
            device_id=device,
            device_id_type=MESH,
        ).start()

    def keep(source, target, sem):
        pltpu.make_async_copy(source, target, sem).start()

    def wait(ref, sem):
        pltpu.make_async_copy(ref, ref, sem).wait()

    x_right = y_hi * X_RING + (x + 1) % X_RING
    x_left = y_hi * X_RING + (x + X_RING - 1) % X_RING
    other = (1 - y_hi) * X_RING + x

    for ref in both:
        pltpu.make_async_copy(ref.m, ref.raw, ref.r_raw.at[0]).start()
    small = ((flags_in, flags, small_sems.at[0]), (logit_in, logit, small_sems.at[1]))
    for source, target, sem in small:
        pltpu.make_async_copy(source, target, sem).start()
    barrier = pltpu.get_barrier_semaphore()

    def greet(to_fsdp, to_shard):
        pl.semaphore_signal(barrier, inc=1, device_id=(to_fsdp, to_shard), device_id_type=MESH)

    greet(fsdp, place(y, z, 1 - core))
    greet(fsdp, place(1 - y, z, core))
    greet(fsdp, place(1 - y, z, 1 - core))
    for to_y in (y, 1 - y):
        for to_core in (core, 1 - core):
            greet(other, place(to_y, z, to_core))
    greet(x_right, shard)
    greet(x_left, shard)

    def greet_z(step, carry):
        greet(fsdp, place(y, (z + step) % Z, core))
        return carry

    lax.fori_loop(1, Z, greet_z, 0)

    for ref in both:
        k = ref.k
        pltpu.make_async_copy(ref.m, ref.raw, ref.r_raw.at[0]).wait()
        for g in range(k.chunks):
            for r in range(k.rows):
                start = (r * k.slabs + g * k.per_chunk) * LANE
                ref.mom[g, :, r * k.span : (r + 1) * k.span] = ref.raw[
                    :, start : start + k.span
                ].astype(BF16)

    pl.semaphore_wait(barrier, 24)

    def to_group(ref, to_core, source, target, s_sem, r_sem):
        @pl.when(core == to_core)
        def _():
            keep(source(y), target, r_sem)

        @pl.when(core != to_core)
        def _():
            send(source(y), target, s_sem, r_sem, (fsdp, place(y, z, to_core)))

        send(source(1 - y), target, s_sem, r_sem, (fsdp, place(1 - y, z, to_core)))

    def rows16(to_y):
        return pl.ds(pl.multiple_of(to_y * 16, 16), 16)

    def gather(g):
        for to_core, ref in enumerate(both):
            if g < ref.k.chunks:
                to_group(
                    ref,
                    to_core,
                    lambda to_y, ref=ref: ref.mom.at[g, rows16(to_y), :],
                    ref.gather.at[g, me],
                    ref.s_gather.at[g],
                    ref.r_gather.at[g],
                )

    def gathered(own, g):
        for ref in both:
            if g < ref.k.chunks:
                strips = ref.mom.at[g, pl.ds(0, 16), :] if ref is own else ref.mom.at[g]
                wait(strips, ref.s_gather.at[g])

    def send_weights():
        for to_core, ref in enumerate(both):
            to_group(
                ref,
                to_core,
                lambda to_y, ref=ref: ref.w.at[rows16(to_y), :],
                ref.weights.at[me],
                ref.s_weights.at[0],
                ref.r_weights.at[0],
            )

    def z_send(rows, source, target, s_sem, r_sem):
        def one(i, carry):
            far = jnp.where(i % 2 == 1, 8 - (i + 1) // 2, 8 + i // 2)
            to_z = (z + far) % Z
            start = pl.multiple_of(to_z * rows, 16)
            send(
                source.at[pl.ds(start, rows), :],
                target.at[pl.ds(pl.multiple_of(z * rows, 16), rows), :],
                s_sem,
                r_sem,
                (fsdp, place(y, to_z, core)),
            )
            return carry

        lax.fori_loop(0, Z - 1, one, 0)
        here = pl.ds(pl.multiple_of(z * rows, 16), rows)
        keep(source.at[here, :], target.at[here, :], r_sem)

    def every(rows, offset):
        return pl.ds(offset, 16, stride=rows)

    def exchange(ref):
        k = ref.k
        rounds = max(kind.chunks for kind in KINDS)
        gather(0)
        for g in range(rounds):
            gathered(ref, g)
            if g + 1 < rounds:
                gather(g + 1)
            if g >= k.chunks:
                continue
            wait(ref.gather.at[g], ref.r_gather.at[g])
            for s in range(4):
                for r in range(k.rows):
                    for c in range(k.per_chunk):
                        start = (r * k.per_chunk + c) * LANE
                        tile = ref.gather[g, s, :, start : start + LANE]
                        ref.turn[every(k.message, c * k.sources + r * 4 + s), :] = tile.astype(F32)
            ref.out_z[g] = ref.turn[...].astype(BF16)
            z_send(k.message, ref.out_z.at[g], ref.in_z.at[g], ref.s_z.at[g], ref.r_z.at[g])

    def orthogonalize(ref):
        k = ref.k
        gram = None
        for g in range(k.chunks):
            wait(ref.in_z.at[g], ref.r_z.at[g])
            ref.turn[...] = ref.in_z[g].astype(F32)
            for c in range(k.per_chunk):
                column = (g * k.per_chunk + c) * LANE
                for n in range(k.sources):
                    tile = ref.turn[every(k.message, c * k.sources + n), :]
                    ref.matrix[n * 16 : n * 16 + 16, column : column + LANE] = tile.astype(BF16)
            part = ref.matrix[:, g * k.span : (g + 1) * k.span]
            term = lax.dot_general(
                part, part, (((1,), (1,)), ((), ())), preferred_element_type=F32
            )
            gram = term if gram is None else gram + term
        return split(newton_schulz(gram, k.size))

    def prepare(ref, terms, g):
        k = ref.k
        high, low = terms
        first, units = k.back[g]
        for i in range(units):
            row, column = divmod((first + i) * UNIT, k.rank)
            own = slice(row * 64, row * 64 + 64)
            both_terms = jnp.concatenate([high[own], low[own]], axis=0)
            both_terms = dot(both_terms, ref.matrix[:, column : column + UNIT])
            update = both_terms[:64] + both_terms[64:]
            for n in range(4):
                for c in range(4):
                    ref.turn[every(units * 16, i * 16 + n * 4 + c), :] = update[
                        n * 16 : n * 16 + 16, c * LANE : (c + 1) * LANE
                    ]
        ref.back_out[back_span(first, units), :] = ref.turn[: Z * units * 16].astype(BF16)

    def start_back(ref, g):
        first, units = ref.k.back[g]
        span = back_span(first, units)
        sems = ref.s_back.at[g], ref.r_back.at[g]
        z_send(units * 16, ref.back_out.at[span, :], ref.back_in.at[span, :], *sems)

    def left_back(ref, g):
        units = ref.k.back[g][1]
        wait(ref.back_out.at[pl.ds(0, (Z - 1) * 16 * units), :], ref.s_back.at[g])

    def back_span(first, units):
        return pl.ds(Z * 16 * first, Z * 16 * units)

    sides = (
        (x_right, lax.rem(x + X_RING - 1, X_RING)),
        (x_left, lax.rem(x + 1, X_RING)),
    )

    def scales():
        ratio = jnp.minimum(1.0, CLIP_TAU / logit[...])
        eta_row = jnp.where(flags[...] > 0, ratio, 1.0)
        spread = jnp.where(identity(32), jnp.broadcast_to(eta_row, (32, 32)), 0.0)
        column = jnp.sum(spread, axis=1, keepdims=True)
        eta = jnp.where(y == 0, column[:16], column[16:])
        return jnp.broadcast_to(eta, (16, LANE)), jnp.broadcast_to(jnp.sqrt(eta), (16, LANE))

    def part(ref, g, start, count):
        rows = pl.ds(pl.multiple_of(start, 16), count)
        return ref.out.at[rows, chunk_columns(ref, g)]

    def chunk_columns(ref, g):
        first, units = ref.k.back[g]
        return slice(first * UNIT, (first + units) * UNIT)

    def renew(ref, g, eta, root):
        k = ref.k
        first, units = k.back[g]
        span = back_span(first, units)
        wait(ref.back_in.at[span, :], ref.r_back.at[g])
        ref.turn[: Z * units * 16] = ref.back_in[span, :].astype(F32)
        tail = eta if k is QUERY else jnp.ones_like(eta)
        for i in range(units):
            for s in range(4):
                row = (first + i) * UNIT // k.rank
                row = ((s // 2) * 32 + z * 2 + s % 2) * k.rows + row
                scale = jnp.where(row < PLAIN, root, tail)
                for c in range(4):
                    update = ref.turn[every(units * 16, i * 16 + s * 4 + c), :]
                    column = (first + i) * UNIT + c * LANE
                    old = ref.weights[s, :, column : column + LANE].astype(F32)
                    fresh = scale * (
                        old * (1.0 - LEARNING_RATE * DECAY_WEIGHT)
                        - LEARNING_RATE * 0.2 * math.sqrt(k.rank) * update
                    )
                    ref.strips[s, :, column : column + LANE] = fresh.astype(BF16)
        columns = chunk_columns(ref, g)
        mine = part(ref, g, fsdp * 32 + y * 16, 16)
        pair = ref.strips.at[pl.ds(pl.multiple_of((1 - y) * 2, 2), 2), :, columns]
        for side, (to_fsdp, _) in enumerate(sides):
            target = ref.cross.at[side, :, :, columns]
            send(pair, target, ref.s_cross.at[g], ref.r_cross.at[g, side], (to_fsdp, shard))
        sems = ref.s_y.at[g], ref.r_y.at[g]
        for to_core in (core, 1 - core):
            strip = ref.strips.at[y * 2 + to_core, :, columns]
            send(strip, mine, *sems, (other, place(y, z, to_core)))
            strip = ref.strips.at[(1 - y) * 2 + to_core, :, columns]
            send(strip, mine, *sems, (fsdp, place(1 - y, z, to_core)))
            send(strip, mine, *sems, (other, place(1 - y, z, to_core)))
        strip = ref.strips.at[y * 2 + 1 - core, :, columns]
        send(strip, mine, *sems, (fsdp, place(y, z, 1 - core)))
        keep(ref.strips.at[me, :, columns], mine, ref.r_y.at[g])

    def pass_on(ref, g):
        columns = chunk_columns(ref, g)
        for side, (_, from_x) in enumerate(sides):
            landed = ref.cross.at[side, :, :, columns]
            wait(landed, ref.r_cross.at[g, side])
            target = part(ref, g, (y_hi * X_RING + from_x) * 32 + y * 16, 16)
            sems = ref.s_pass.at[g], ref.r_pass.at[g, side]
            for to_core in range(2):
                strip = ref.cross.at[side, to_core, :, columns]
                for to_fsdp in (fsdp, other):
                    send(strip, target, *sems, (to_fsdp, place(1 - y, z, to_core)))

    def along_x(ref, g):
        wait(part(ref, g, 0, 64), ref.r_y.at[g])
        for h in range(2):
            rows = part(ref, g, (h * X_RING + x) * 32 + y * 16, 16)
            for side, (to_fsdp, _) in enumerate(sides):
                send(rows, rows, ref.s_x.at[g], ref.r_x.at[g, side], (to_fsdp, shard))

    def relay(ref, g):
        for side, (to_fsdp, from_x) in enumerate(sides):
            wait(part(ref, g, 0, 32), ref.r_x.at[g, side])
            wait(part(ref, g, 0, 32), ref.r_pass.at[g, side])
            rows = part(ref, g, (side * X_RING + from_x) * 32, 32)
            send(rows, rows, ref.s_x.at[g], ref.r_relay.at[g, side], (to_fsdp, shard))

    def run(ref):
        k = ref.k
        exchange(ref)
        send_weights()
        terms = orthogonalize(ref)
        prepare(ref, terms, 0)
        start_back(ref, 0)
        prepare(ref, terms, 1)
        for source, target, sem in small:
            pltpu.make_async_copy(source, target, sem).wait()
        eta, root = scales()
        wait(ref.weights, ref.r_weights.at[0])
        left_back(ref, 0)
        start_back(ref, 1)
        if k is KEYVAL:
            renew(kv, 0, eta, root)
            pass_on(kv, 0)
            along_x(kv, 0)
            renew(kv, 1, eta, root)
            pass_on(kv, 1)
            along_x(kv, 1)
            relay(kv, 0)
            along_x(q, 0)
            relay(kv, 1)
            along_x(q, 1)
            relay(q, 0)
        else:
            prepare(q, terms, 2)
            prepare(q, terms, 3)
            along_x(kv, 0)
            renew(q, 0, eta, root)
            along_x(kv, 1)
            relay(kv, 0)
            left_back(q, 1)
            start_back(q, 2)
            start_back(q, 3)
            pass_on(q, 0)
            along_x(q, 0)
            renew(q, 1, eta, root)
            relay(kv, 1)
            pass_on(q, 1)
            renew(q, 2, eta, root)
            along_x(q, 1)
            renew(q, 3, eta, root)
            relay(q, 0)
            pass_on(q, 2)
            pass_on(q, 3)
        along_x(q, 2)
        along_x(q, 3)
        relay(q, 1)
        relay(q, 2)
        relay(q, 3)
        for g in range(2 if k is QUERY else 1, len(k.back)):
            left_back(ref, g)
        for g in range(len(k.back)):
            wait(part(ref, g, 0, 112), ref.s_y.at[g])
            wait(part(ref, g, 0, 64), ref.s_cross.at[g])
            wait(part(ref, g, 0, 128), ref.s_pass.at[g])
        for g in range(k.chunks):
            most = pl.ds(0, (Z - 1) * k.message)
            wait(ref.out_z.at[g, most, :], ref.s_z.at[g])
        wait(ref.weights.at[0], ref.s_weights.at[0])
        away = kv if ref is q else q
        wait(away.weights.at[pl.ds(0, 2)], away.s_weights.at[0])

    pl.when(core == 0)(lambda: run(q))
    pl.when(core == 1)(lambda: run(kv))

    for ref in both:
        for g in range(len(ref.k.back)):
            wait(part(ref, g, 0, 32), ref.r_relay.at[g, 0])
            wait(part(ref, g, 0, 32), ref.r_relay.at[g, 1])
            wait(part(ref, g, 0, 128), ref.s_x.at[g])


def per_device(
    query_momentum, key_value_momentum, query_blocks, key_value_blocks, clip_flags, logit_max
):
    hbm = pl.BlockSpec(memory_space=pltpu.HBM)
    anywhere = pl.BlockSpec(memory_space=pl.ANY)
    scratch = [
        pltpu.VMEM((1, 32), jnp.int32),
        pltpu.VMEM((1, 32), F32),
        pltpu.SemaphoreType.DMA((2,)),
    ]
    for k in KINDS:
        scratch += list(scratch_of(k).values())
    return pl.pallas_call(
        kernel,
        name="muon",
        out_shape=tuple(pltpu.VMEM((256, k.piece), BF16) for k in KINDS),
        in_specs=[hbm] * 6,
        out_specs=(anywhere, anywhere),
        scratch_shapes=scratch,
        compiler_params=pltpu.CompilerParams(
            collective_id=0, has_side_effects=True, vmem_limit_bytes=60 * 1024 * 1024
        ),
    )(
        query_momentum,
        key_value_momentum,
        query_blocks,
        key_value_blocks,
        clip_flags.reshape(1, 32),
        logit_max.reshape(1, 32),
    )


def solution(mesh):
    placed = (
        P("fsdp", "shard"),
        P("fsdp", "shard"),
        P("fsdp", "shard"),
        P("fsdp", "shard"),
        P("fsdp"),
        P("fsdp"),
    )
    return jax.shard_map(
        per_device,
        mesh=mesh,
        in_specs=placed,
        out_specs=(P(None, "shard"), P(None, "shard")),
        check_vma=False,
    )
```

```python
import functools
import math
from types import SimpleNamespace

import jax
import jax.numpy as jnp
from jax import lax
from jax.experimental import pallas as pl
from jax.experimental.pallas import tpu as pltpu
from jax.sharding import PartitionSpec as P

COEF_A = 3.4445
COEF_B = -4.775
COEF_C = 2.0315
CLIP_TAU = 100.0
LEARNING_RATE = 0.5
DECAY_WEIGHT = 0.1
NS_ITERS = 5
PLAIN = 128

F32 = jnp.float32
BF16 = jnp.bfloat16
Z = 16
LANE = 128
X_RING = 4
MESH = pl.DeviceIdType.MESH


def make_kind(name, rows, rank, chunks, back):
    slabs = rank // LANE
    per_chunk = slabs // chunks
    sources = 4 * rows
    return SimpleNamespace(
        name=name,
        rows=rows,
        rank=rank,
        chunks=chunks,
        slabs=slabs,
        per_chunk=per_chunk,
        sources=sources,
        message=sources * per_chunk,
        size=Z * sources,
        piece=rows * rank,
        strip=rows * per_chunk * LANE,
        span=per_chunk * LANE,
        back=tuple((sum(back[:i]), n) for i, n in enumerate(back)),
    )


UNIT = 512
QUERY = make_kind("q", 3, 1536, 3, (2, 3, 3, 1))
KEYVAL = make_kind("kv", 4, 512, 2, (2, 2))
KINDS = (QUERY, KEYVAL)


def scratch_of(kind):
    g, b = kind.chunks, len(kind.back)
    back_size = Z * 4 * kind.piece // LANE
    dma = pltpu.SemaphoreType.DMA
    return dict(
        raw=pltpu.VMEM((32, kind.piece), F32),
        mom=pltpu.VMEM((g, 32, kind.strip), BF16),
        gather=pltpu.VMEM((g, 4, 16, kind.strip), BF16),
        weights=pltpu.VMEM((4, 16, kind.piece), BF16),
        turn=pltpu.VMEM((Z * kind.message, LANE), F32),
        out_z=pltpu.VMEM((g, Z * kind.message, LANE), BF16),
        in_z=pltpu.VMEM((g, Z * kind.message, LANE), BF16),
        back_out=pltpu.VMEM((back_size, LANE), BF16),
        back_in=pltpu.VMEM((back_size, LANE), BF16),
        matrix=pltpu.VMEM((kind.size, kind.rank), BF16),
        strips=pltpu.VMEM((4, 16, kind.piece), BF16),
        r_raw=dma((1,)),
        cross=pltpu.VMEM((2, 2, 16, kind.piece), BF16),
        s_cross=dma((b,)),
        r_cross=dma((b, 2)),
        s_pass=dma((b,)),
        r_pass=dma((b, 2)),
        s_gather=dma((g,)),
        r_gather=dma((g,)),
        s_weights=dma((1,)),
        r_weights=dma((1,)),
        s_z=dma((g,)),
        r_z=dma((g,)),
        s_back=dma((b,)),
        r_back=dma((b,)),
        s_y=dma((b,)),
        r_y=dma((b,)),
        s_x=dma((b,)),
        r_x=dma((b, 2)),
        r_relay=dma((b, 2)),
    )


NAMES = tuple(scratch_of(QUERY))


def split(value):
    high = value.astype(BF16)
    return high, (value - high.astype(F32)).astype(BF16)


def dot(left, right):
    return jnp.dot(left, right, preferred_element_type=F32)


def product(left, right):
    return dot(left[0], right[0]) + (dot(left[0], right[1]) + dot(left[1], right[0]))


def identity(size):
    first = lax.broadcasted_iota(jnp.int32, (size, size), 0)
    second = lax.broadcasted_iota(jnp.int32, (size, size), 1)
    return first == second


def newton_schulz(gram, size):
    diagonal = identity(size)
    square = jnp.sum(jnp.where(diagonal, gram, 0.0), axis=(0, 1), keepdims=True)
    inverse = 1.0 / (jnp.sqrt(square) + 1e-07)
    a = (gram * inverse) * inverse
    total = None
    for step in range(NS_ITERS):
        a_parts = split(a)
        poly = COEF_B * a + COEF_C * product(a_parts, a_parts)
        poly = jnp.where(diagonal, poly + COEF_A, poly)
        parts = split(poly)
        total = poly if total is None else product(parts, split(total))
        if step < NS_ITERS - 1:
            a = product(parts, split(product(parts, a_parts)))
    return total * inverse


def kernel(q_mom, kv_mom, q_weights, kv_weights, flags_in, logit_in, q_out, kv_out, *scratch):
    flags, logit, small_sems, *scratch = scratch
    fsdp = lax.axis_index("fsdp")
    shard = lax.axis_index("shard")
    y_hi, x = fsdp // X_RING, fsdp % X_RING
    y, z, core = shard // 32, (shard // 2) % Z, shard % 2
    me = y * 2 + core
    half = len(NAMES)
    q = SimpleNamespace(
        k=QUERY, m=q_mom, w=q_weights, out=q_out, **dict(zip(NAMES, scratch[:half]))
    )
    kv = SimpleNamespace(
        k=KEYVAL, m=kv_mom, w=kv_weights, out=kv_out, **dict(zip(NAMES, scratch[half:]))
    )
    both = (q, kv)

    def place(to_y, to_z, to_core):
        return to_y * 32 + to_z * 2 + to_core

    def send(source, target, s_sem, r_sem, device):
        pltpu.make_async_remote_copy(
            src_ref=source,
            dst_ref=target,
            send_sem=s_sem,
            recv_sem=r_sem,
            device_id=device,
            device_id_type=MESH,
        ).start()

    def keep(source, target, sem):
        pltpu.make_async_copy(source, target, sem).start()

    def wait(ref, sem):
        pltpu.make_async_copy(ref, ref, sem).wait()

    x_right = y_hi * X_RING + (x + 1) % X_RING
    x_left = y_hi * X_RING + (x + X_RING - 1) % X_RING
    other = (1 - y_hi) * X_RING + x

    for ref in both:
        pltpu.make_async_copy(ref.m, ref.raw, ref.r_raw.at[0]).start()
    small = ((flags_in, flags, small_sems.at[0]), (logit_in, logit, small_sems.at[1]))
    for source, target, sem in small:
        pltpu.make_async_copy(source, target, sem).start()
    barrier = pltpu.get_barrier_semaphore()

    def greet(to_fsdp, to_shard):
        pl.semaphore_signal(barrier, inc=1, device_id=(to_fsdp, to_shard), device_id_type=MESH)

    greet(fsdp, place(y, z, 1 - core))
    greet(fsdp, place(1 - y, z, core))
    greet(fsdp, place(1 - y, z, 1 - core))
    for to_y in (y, 1 - y):
        for to_core in (core, 1 - core):
            greet(other, place(to_y, z, to_core))
    greet(x_right, shard)
    greet(x_left, shard)

    def greet_z(step, carry):
        greet(fsdp, place(y, (z + step) % Z, core))
        return carry

    lax.fori_loop(1, Z, greet_z, 0)

    for ref in both:
        k = ref.k
        pltpu.make_async_copy(ref.m, ref.raw, ref.r_raw.at[0]).wait()
        for g in range(k.chunks):
            for r in range(k.rows):
                start = (r * k.slabs + g * k.per_chunk) * LANE
                ref.mom[g, :, r * k.span : (r + 1) * k.span] = ref.raw[
                    :, start : start + k.span
                ].astype(BF16)

    pl.semaphore_wait(barrier, 24)

    def to_group(ref, to_core, source, target, s_sem, r_sem):
        @pl.when(core == to_core)
        def _():
            keep(source(y), target, r_sem)

        @pl.when(core != to_core)
        def _():
            send(source(y), target, s_sem, r_sem, (fsdp, place(y, z, to_core)))

        send(source(1 - y), target, s_sem, r_sem, (fsdp, place(1 - y, z, to_core)))

    def rows16(to_y):
        return pl.ds(pl.multiple_of(to_y * 16, 16), 16)

    def gather(g):
        for to_core, ref in enumerate(both):
            if g < ref.k.chunks:
                to_group(
                    ref,
                    to_core,
                    lambda to_y, ref=ref: ref.mom.at[g, rows16(to_y), :],
                    ref.gather.at[g, me],
                    ref.s_gather.at[g],
                    ref.r_gather.at[g],
                )

    def gathered(own, g):
        for ref in both:
            if g < ref.k.chunks:
                strips = ref.mom.at[g, pl.ds(0, 16), :] if ref is own else ref.mom.at[g]
                wait(strips, ref.s_gather.at[g])

    def send_weights():
        for to_core, ref in enumerate(both):
            to_group(
                ref,
                to_core,
                lambda to_y, ref=ref: ref.w.at[rows16(to_y), :],
                ref.weights.at[me],
                ref.s_weights.at[0],
                ref.r_weights.at[0],
            )

    def z_send(rows, source, target, s_sem, r_sem):
        def one(i, carry):
            far = jnp.where(i % 2 == 1, 8 - (i + 1) // 2, 8 + i // 2)
            to_z = (z + far) % Z
            start = pl.multiple_of(to_z * rows, 16)
            send(
                source.at[pl.ds(start, rows), :],
                target.at[pl.ds(pl.multiple_of(z * rows, 16), rows), :],
                s_sem,
                r_sem,
                (fsdp, place(y, to_z, core)),
            )
            return carry

        lax.fori_loop(0, Z - 1, one, 0)
        here = pl.ds(pl.multiple_of(z * rows, 16), rows)
        keep(source.at[here, :], target.at[here, :], r_sem)

    def every(rows, offset):
        return pl.ds(offset, 16, stride=rows)

    def exchange(ref):
        k = ref.k
        rounds = max(kind.chunks for kind in KINDS)
        gather(0)
        for g in range(rounds):
            gathered(ref, g)
            if g + 1 < rounds:
                gather(g + 1)
            if g >= k.chunks:
                continue
            wait(ref.gather.at[g], ref.r_gather.at[g])
            for s in range(4):
                for r in range(k.rows):
                    for c in range(k.per_chunk):
                        start = (r * k.per_chunk + c) * LANE
                        tile = ref.gather[g, s, :, start : start + LANE]
                        ref.turn[every(k.message, c * k.sources + r * 4 + s), :] = tile.astype(F32)
            ref.out_z[g] = ref.turn[...].astype(BF16)
            z_send(k.message, ref.out_z.at[g], ref.in_z.at[g], ref.s_z.at[g], ref.r_z.at[g])

    def orthogonalize(ref):
        k = ref.k
        gram = None
        for g in range(k.chunks):
            wait(ref.in_z.at[g], ref.r_z.at[g])
            ref.turn[...] = ref.in_z[g].astype(F32)
            for c in range(k.per_chunk):
                column = (g * k.per_chunk + c) * LANE
                for n in range(k.sources):
                    tile = ref.turn[every(k.message, c * k.sources + n), :]
                    ref.matrix[n * 16 : n * 16 + 16, column : column + LANE] = tile.astype(BF16)
            part = ref.matrix[:, g * k.span : (g + 1) * k.span]
            term = lax.dot_general(
                part, part, (((1,), (1,)), ((), ())), preferred_element_type=F32
            )
            gram = term if gram is None else gram + term
        return split(newton_schulz(gram, k.size))

    def prepare(ref, terms, g):
        k = ref.k
        high, low = terms
        first, units = k.back[g]
        for i in range(units):
            row, column = divmod((first + i) * UNIT, k.rank)
            own = slice(row * 64, row * 64 + 64)
            both_terms = jnp.concatenate([high[own], low[own]], axis=0)
            both_terms = dot(both_terms, ref.matrix[:, column : column + UNIT])
            update = both_terms[:64] + both_terms[64:]
            for n in range(4):
                for c in range(4):
                    ref.turn[every(units * 16, i * 16 + n * 4 + c), :] = update[
                        n * 16 : n * 16 + 16, c * LANE : (c + 1) * LANE
                    ]
        ref.back_out[back_span(first, units), :] = ref.turn[: Z * units * 16].astype(BF16)

    def start_back(ref, g):
        first, units = ref.k.back[g]
        span = back_span(first, units)
        sems = ref.s_back.at[g], ref.r_back.at[g]
        z_send(units * 16, ref.back_out.at[span, :], ref.back_in.at[span, :], *sems)

    def left_back(ref, g):
        units = ref.k.back[g][1]
        wait(ref.back_out.at[pl.ds(0, (Z - 1) * 16 * units), :], ref.s_back.at[g])

    def back_span(first, units):
        return pl.ds(Z * 16 * first, Z * 16 * units)

    sides = (
        (x_right, lax.rem(x + X_RING - 1, X_RING)),
        (x_left, lax.rem(x + 1, X_RING)),
    )

    def scales():
        ratio = jnp.minimum(1.0, CLIP_TAU / logit[...])
        eta_row = jnp.where(flags[...] > 0, ratio, 1.0)
        spread = jnp.where(identity(32), jnp.broadcast_to(eta_row, (32, 32)), 0.0)
        column = jnp.sum(spread, axis=1, keepdims=True)
        eta = jnp.where(y == 0, column[:16], column[16:])
        return jnp.broadcast_to(eta, (16, LANE)), jnp.broadcast_to(jnp.sqrt(eta), (16, LANE))

    def part(ref, g, start, count):
        rows = pl.ds(pl.multiple_of(start, 16), count)
        return ref.out.at[rows, chunk_columns(ref, g)]

    def chunk_columns(ref, g):
        first, units = ref.k.back[g]
        return slice(first * UNIT, (first + units) * UNIT)

    def renew(ref, g, eta, root):
        k = ref.k
        first, units = k.back[g]
        span = back_span(first, units)
        wait(ref.back_in.at[span, :], ref.r_back.at[g])
        ref.turn[: Z * units * 16] = ref.back_in[span, :].astype(F32)
        tail = eta if k is QUERY else jnp.ones_like(eta)
        for i in range(units):
            for s in range(4):
                row = (first + i) * UNIT // k.rank
                row = ((s // 2) * 32 + z * 2 + s % 2) * k.rows + row
                scale = jnp.where(row < PLAIN, root, tail)
                for c in range(4):
                    update = ref.turn[every(units * 16, i * 16 + s * 4 + c), :]
                    column = (first + i) * UNIT + c * LANE
                    old = ref.weights[s, :, column : column + LANE].astype(F32)
                    fresh = scale * (
                        old * (1.0 - LEARNING_RATE * DECAY_WEIGHT)
                        - LEARNING_RATE * 0.2 * math.sqrt(k.rank) * update
                    )
                    ref.strips[s, :, column : column + LANE] = fresh.astype(BF16)
        columns = chunk_columns(ref, g)
        mine = part(ref, g, fsdp * 32 + y * 16, 16)
        pair = ref.strips.at[pl.ds(pl.multiple_of((1 - y) * 2, 2), 2), :, columns]
        for side, (to_fsdp, _) in enumerate(sides):
            target = ref.cross.at[side, :, :, columns]
            send(pair, target, ref.s_cross.at[g], ref.r_cross.at[g, side], (to_fsdp, shard))
        sems = ref.s_y.at[g], ref.r_y.at[g]
        for to_core in (core, 1 - core):
            strip = ref.strips.at[y * 2 + to_core, :, columns]
            send(strip, mine, *sems, (other, place(y, z, to_core)))
            strip = ref.strips.at[(1 - y) * 2 + to_core, :, columns]
            send(strip, mine, *sems, (fsdp, place(1 - y, z, to_core)))
            send(strip, mine, *sems, (other, place(1 - y, z, to_core)))
        strip = ref.strips.at[y * 2 + 1 - core, :, columns]
        send(strip, mine, *sems, (fsdp, place(y, z, 1 - core)))
        keep(ref.strips.at[me, :, columns], mine, ref.r_y.at[g])

    def pass_on(ref, g):
        columns = chunk_columns(ref, g)
        for side, (_, from_x) in enumerate(sides):
            landed = ref.cross.at[side, :, :, columns]
            wait(landed, ref.r_cross.at[g, side])
            target = part(ref, g, (y_hi * X_RING + from_x) * 32 + y * 16, 16)
            sems = ref.s_pass.at[g], ref.r_pass.at[g, side]
            for to_core in range(2):
                strip = ref.cross.at[side, to_core, :, columns]
                for to_fsdp in (fsdp, other):
                    send(strip, target, *sems, (to_fsdp, place(1 - y, z, to_core)))

    def along_x(ref, g):
        wait(part(ref, g, 0, 64), ref.r_y.at[g])
        for h in range(2):
            rows = part(ref, g, (h * X_RING + x) * 32 + y * 16, 16)
            for side, (to_fsdp, _) in enumerate(sides):
                send(rows, rows, ref.s_x.at[g], ref.r_x.at[g, side], (to_fsdp, shard))

    def relay(ref, g):
        for side, (to_fsdp, from_x) in enumerate(sides):
            wait(part(ref, g, 0, 32), ref.r_x.at[g, side])
            wait(part(ref, g, 0, 32), ref.r_pass.at[g, side])
            rows = part(ref, g, (side * X_RING + from_x) * 32, 32)
            send(rows, rows, ref.s_x.at[g], ref.r_relay.at[g, side], (to_fsdp, shard))

    def run(ref):
        k = ref.k
        exchange(ref)
        send_weights()
        terms = orthogonalize(ref)
        prepare(ref, terms, 0)
        start_back(ref, 0)
        prepare(ref, terms, 1)
        for source, target, sem in small:
            pltpu.make_async_copy(source, target, sem).wait()
        eta, root = scales()
        wait(ref.weights, ref.r_weights.at[0])
        left_back(ref, 0)
        start_back(ref, 1)
        if k is KEYVAL:
            renew(kv, 0, eta, root)
            pass_on(kv, 0)
            along_x(kv, 0)
            renew(kv, 1, eta, root)
            pass_on(kv, 1)
            along_x(kv, 1)
            relay(kv, 0)
            along_x(q, 0)
            relay(kv, 1)
            along_x(q, 1)
            relay(q, 0)
        else:
            prepare(q, terms, 2)
            prepare(q, terms, 3)
            along_x(kv, 0)
            renew(q, 0, eta, root)
            along_x(kv, 1)
            relay(kv, 0)
            left_back(q, 1)
            start_back(q, 2)
            start_back(q, 3)
            pass_on(q, 0)
            along_x(q, 0)
            renew(q, 1, eta, root)
            relay(kv, 1)
            pass_on(q, 1)
            renew(q, 2, eta, root)
            along_x(q, 1)
            renew(q, 3, eta, root)
            relay(q, 0)
            pass_on(q, 2)
            pass_on(q, 3)
        along_x(q, 2)
        along_x(q, 3)
        relay(q, 1)
        relay(q, 2)
        relay(q, 3)
        for g in range(2 if k is QUERY else 1, len(k.back)):
            left_back(ref, g)
        for g in range(len(k.back)):
            wait(part(ref, g, 0, 112), ref.s_y.at[g])
            wait(part(ref, g, 0, 64), ref.s_cross.at[g])
            wait(part(ref, g, 0, 128), ref.s_pass.at[g])
        for g in range(k.chunks):
            most = pl.ds(0, (Z - 1) * k.message)
            wait(ref.out_z.at[g, most, :], ref.s_z.at[g])
        wait(ref.weights.at[0], ref.s_weights.at[0])
        away = kv if ref is q else q
        wait(away.weights.at[pl.ds(0, 2)], away.s_weights.at[0])

    pl.when(core == 0)(lambda: run(q))
    pl.when(core == 1)(lambda: run(kv))

    for ref in both:
        for g in range(len(ref.k.back)):
            wait(part(ref, g, 0, 32), ref.r_relay.at[g, 0])
            wait(part(ref, g, 0, 32), ref.r_relay.at[g, 1])
            wait(part(ref, g, 0, 128), ref.s_x.at[g])


def per_device(
    query_momentum, key_value_momentum, query_blocks, key_value_blocks, clip_flags, logit_max
):
    hbm = pl.BlockSpec(memory_space=pltpu.HBM)
    anywhere = pl.BlockSpec(memory_space=pl.ANY)
    scratch = [
        pltpu.VMEM((1, 32), jnp.int32),
        pltpu.VMEM((1, 32), F32),
        pltpu.SemaphoreType.DMA((2,)),
    ]
    for k in KINDS:
        scratch += list(scratch_of(k).values())
    return pl.pallas_call(
        kernel,
        name="muon",
        out_shape=tuple(pltpu.VMEM((256, k.piece), BF16) for k in KINDS),
        in_specs=[hbm] * 6,
        out_specs=(anywhere, anywhere),
        scratch_shapes=scratch,
        compiler_params=pltpu.CompilerParams(
            collective_id=0, has_side_effects=True, vmem_limit_bytes=60 * 1024 * 1024
        ),
    )(
        query_momentum,
        key_value_momentum,
        query_blocks,
        key_value_blocks,
        clip_flags.reshape(1, 32),
        logit_max.reshape(1, 32),
    )


def solution(mesh):
    placed = (
        P("fsdp", "shard"),
        P("fsdp", "shard"),
        P("fsdp", "shard"),
        P("fsdp", "shard"),
        P("fsdp"),
        P("fsdp"),
    )
    return jax.shard_map(
        per_device,
        mesh=mesh,
        in_specs=placed,
        out_specs=(P(None, "shard"), P(None, "shard")),
        check_vma=False,
    )
```
